256 devices in a mesh: rows: 32 (over y_hi, z, core), cols: 8 (over x, y_lo).
Axes of the slice: x: 4, y: 4 (y_hi: 2, y_lo: 2; y = y_hi * 2 + y_lo), z: 8, core: 2. Of those that a mesh axis runs over, the one named last changes fastest.
Arguments:
- codes: int32 [512, 393216], P('cols', 'rows'), may hold values from 0 to 63
- labels: int32 [393216], P('rows'), may hold values 0 or 1
- base_margin: float32 [393216], P('rows'), may hold values from -6 to 6
- node_id: int32 [393216], P('rows'), may hold values from 0 to 15
- split_feature: int32 [256], replicated, may hold values from 0 to 511
- threshold: int32 [256], replicated, may hold values from 0 to 62
- leaf_value: float32 [256], replicated, may hold values from -6 to 6
Outputs:
- split_gains: float32 [16, 32768], P(None, ('cols', 'rows'))
- best_gain: float32 [16], replicated
The draws below stay inside these ranges and needn't reach their ends.
All inputs are finite; a program needn't handle non-finite values. No bound on the sum of `labels` on one device may be relied on, other than what follows from the above.
Results may differ from the reference program's by a relative error of at most 0.0015.
Values may be sent and summed in bfloat16 or wider, within the bound.
A program may use at most 64 MiB of HBM per device.

```python
import jax
import jax.numpy as jnp
from jax import lax

FEATURES = 512
BINS = 64
NODES = 16
DEPTH = 8
TREE_NODES = 256
SAMPLES = 393216


def place_ends(array, stream_key, least, largest):
    extent = array.shape
    index_at = [jax.random.randint(jax.random.fold_in(stream_key, axis), (), 0, extent[axis]) for axis in range(len(extent))]
    array = array.at[tuple(index_at)].set(least)
    longest = extent.index(max(extent))
    index_at[longest] = (index_at[longest] + 1) % extent[longest]
    return array.at[tuple(index_at)].set(largest)


def level_of(stream_key, dims, cuts, smallest, top_value):
    factor_of = 1.0
    for dim, parts in cuts:
        draws = jax.random.uniform(jax.random.fold_in(jax.random.fold_in(stream_key, 6), dim), (parts,), jnp.float32, smallest / len(cuts), top_value / len(cuts))
        factor_of = factor_of * jnp.repeat(jnp.exp(draws), dims[dim] // parts).reshape((-1,) + (1,) * (len(dims) - 1 - dim))
    return factor_of


def centred(stream_key, dims, scale, limit, shards=(), held_as=jnp.bfloat16):
    drawn = scale * jax.random.normal(stream_key, dims, jnp.float32)
    if shards:
        drawn = drawn * level_of(stream_key, dims, shards, -0.22, 0.18)
    return jnp.clip(drawn, -limit, limit).astype(held_as)


def setup_inputs(seed: int = 0) -> dict:
    keys = jax.random.split(jax.random.key(seed), 8)
    return {
        "codes": place_ends(jax.random.randint(keys[0], (FEATURES, SAMPLES), 0, BINS), jax.random.fold_in(keys[0], 1), 0, BINS - 1).astype(jnp.int32),
        "labels": place_ends((jax.random.randint(keys[1], (SAMPLES,), 0, 2) < 1).astype(jnp.int32), jax.random.fold_in(keys[1], 1), 0, 1),
        "base_margin": centred(keys[2], (SAMPLES,), 1.0, 6.0, ((0, 32),), jnp.float32),
        "node_id": place_ends(jax.random.randint(keys[3], (SAMPLES,), 0, NODES), jax.random.fold_in(keys[3], 1), 0, NODES - 1).astype(jnp.int32),
        "split_feature": place_ends(jax.random.randint(keys[4], (TREE_NODES,), 0, FEATURES), jax.random.fold_in(keys[4], 1), 0, FEATURES - 1).astype(jnp.int32),
        "threshold": place_ends(jax.random.randint(keys[5], (TREE_NODES,), 0, BINS - 1), jax.random.fold_in(keys[5], 1), 0, (BINS - 1) - 1).astype(jnp.int32),
        "leaf_value": centred(keys[6], (TREE_NODES,), 1.0, 6.0, (), jnp.float32),
    }


reg_lambda = 1.0


def reference(codes, labels, base_margin, node_id, split_feature, threshold, leaf_value):
    picked = jnp.take(codes, split_feature, axis=0)
    node_index = jnp.ones((SAMPLES,), jnp.int32)
    for depth_level in range(DEPTH):
        chosen = jnp.take_along_axis(picked, node_index[None, :], axis=0)[0]
        go_right = (chosen > threshold[node_index]).astype(jnp.int32)
        node_index = 2 * node_index + go_right
    margin = base_margin + leaf_value[node_index - TREE_NODES]
    probability = jax.nn.sigmoid(margin)
    gradient = (probability - labels.astype(jnp.float32)).astype(jnp.bfloat16)
    hessian = (probability * (1.0 - probability)).astype(jnp.bfloat16)
    gradient = lax.optimization_barrier(gradient).astype(jnp.float32)
    hessian = lax.optimization_barrier(hessian).astype(jnp.float32)

    def feature_hist(feature):
        column = lax.dynamic_slice_in_dim(codes, feature, 1, 0)[0]
        segment = node_id * BINS + column
        grad_part = jax.ops.segment_sum(gradient, segment, num_segments=NODES * BINS)
        hess_part = jax.ops.segment_sum(hessian, segment, num_segments=NODES * BINS)
        return grad_part, hess_part

    grad_hist, hess_hist = lax.map(feature_hist, jnp.arange(FEATURES, dtype=jnp.int32))
    grad_hist = jnp.transpose(grad_hist.reshape(FEATURES, NODES, BINS), (1, 0, 2))
    hess_hist = jnp.transpose(hess_hist.reshape(FEATURES, NODES, BINS), (1, 0, 2))
    grad_left = jnp.cumsum(grad_hist, axis=2)
    hess_left = jnp.cumsum(hess_hist, axis=2)
    grad_node = grad_left[:, :, -1:]
    hess_node = hess_left[:, :, -1:]
    grad_right = grad_node - grad_left
    hess_right = hess_node - hess_left
    split_score = 0.5 * (grad_left * grad_left / (hess_left + reg_lambda)
                         + grad_right * grad_right / (hess_right + reg_lambda)
                         - grad_node * grad_node / (hess_node + reg_lambda))
    split_gains = split_score.reshape(NODES, FEATURES * BINS)
    best_gain = jnp.max(split_gains, axis=1)
    return split_gains, best_gain
```

```python
import functools

import jax
import jax.numpy as jnp
from jax import lax
from jax.experimental import pallas as pl
from jax.experimental.pallas import tpu as pltpu
from jax.sharding import PartitionSpec as P

BINS = 64
NODES = 16
SUB = 16
PIECES = 8
GROUP = 4
reg_lambda = 1.0
MESH = pl.DeviceIdType.MESH
F32, BF16, F8, I8 = jnp.float32, jnp.bfloat16, jnp.float8_e4m3fn, jnp.int8


def walk(bits):
    rows = lax.broadcasted_iota(jnp.int32, bits.shape, 0)
    slot = jnp.ones((1, bits.shape[1]), jnp.int32)
    for _ in range(4):
        bit = jnp.sum(jnp.where(rows == slot, bits, 0.0), axis=0, keepdims=True)
        slot = 2 * slot + bit.astype(jnp.int32)
    return slot


def pieces_of(value):
    scaled = value * 2048.0
    whole = jnp.floor(scaled + 0.5)
    rest = (scaled - whole) * 256.0
    digits = []
    for _ in range(5):
        upper = jnp.floor(whole * 0.25 + 0.5)
        digits.append(whole - 4.0 * upper)
        whole = upper
    digits.append(whole)
    wide = rest * 1048577.0
    top = wide - (wide - rest)
    return digits + [top, (rest - top) * 16.0]


PIECE_SCALES = [4.0**i / 2048.0 for i in range(6)] + [2.0**-19, 2.0**-23]


def kernel(
    cols, chips,
    codes_ref, labels_ref, base_ref, node_ref, sf_ref, thr_ref, sfp_ref, thrp_ref, leaf_ref,
    gains_ref, best_ref,
    aug, cs, tab, sA, rA, sB, rB, subs, ps, W, pair_s, pair_r, hs, hr, m1s, m1r, m2s, m2r,
    semA, semS, semB, semP, semX, semH, semM, semN,
):
    feats, samples = codes_ref.shape
    C = samples // cols
    me = lax.axis_index("cols")
    row = lax.axis_index("rows")
    chip, core = row // 2, lax.rem(row, 2)

    def col_of(k):
        return lax.rem(me + k, cols)

    def chip_of(k):
        return lax.rem(chip + k, chips)

    def chunk(c):
        return pl.ds(pl.multiple_of(c * C, C), C)

    barrier = pltpu.get_barrier_semaphore()

    def greet(r, c):
        pl.semaphore_signal(barrier, inc=1, device_id=(r, c), device_id_type=MESH)

    for k in range(1, cols):
        greet(row, col_of(k))
    for k in range(cols):
        greet(chip * 2 + 1 - core, col_of(k))
    for k in range(1, chips):
        greet(chip_of(k) * 2 + core, me)

    aug[0:feats, :] = codes_ref[...].astype(BF16)
    aug[feats:, :] = jnp.where(lax.broadcasted_iota(jnp.int32, (16, samples), 0) == 0, 1.0, 0.0).astype(BF16)
    for g in range(chips):
        cs[g] = codes_ref[GROUP * g : GROUP * (g + 1), :].astype(I8)

    ids = lax.broadcasted_iota(jnp.int32, (feats, 256), 0) + me * feats
    last = lax.broadcasted_iota(jnp.int32, (16, 256), 0) == 0

    def selector(features, bounds):
        one = jnp.where(features == ids, 1.0, 0.0)
        low = jnp.where(last, -bounds.astype(F32), 0.0)
        return jnp.concatenate([one, low], axis=0).T.astype(BF16)

    top = selector(sf_ref[...], thr_ref[...])[0:SUB]
    deep = selector(sfp_ref[...], thrp_ref[...])

    pl.semaphore_wait(barrier, (cols - 1) + cols + (chips - 1))

    def to_cols(src, dst, sem, k):
        return pltpu.make_async_remote_copy(
            src_ref=src, dst_ref=dst, send_sem=sem.at[0, k], recv_sem=sem.at[1, k],
            device_id=(row, col_of(k)), device_id_type=MESH,
        )

    def top_bits(c):
        t = jnp.dot(top, aug[:, chunk(c)], preferred_element_type=F32)
        return jnp.where(t > 0.0, 1.0, 0.0).astype(BF16)

    def stepA(k, _):
        sA[k] = top_bits(col_of(k))
        to_cols(sA.at[k], rA.at[k], semA, k).start()
        return 0

    lax.fori_loop(1, cols, stepA, 0)
    rA[0] = top_bits(me)

    def table(c, _):
        tab[:, chunk(c)] = jnp.dot(deep, aug[:, chunk(c)], preferred_element_type=F32).astype(BF16)
        return 0

    lax.fori_loop(0, cols, table, 0)

    def waits(src, dst, sem):
        def w(k, _):
            to_cols(src.at[k], dst.at[k], sem, k).wait_recv()
            return 0

        lax.fori_loop(1, cols, w, 0)

    def sends(src, dst, sem):
        def w(k, _):
            to_cols(src.at[k], dst.at[k], sem, k).wait_send()
            return 0

        lax.fori_loop(1, cols, w, 0)

    def total(ref):
        s = ref[0].astype(F32)
        for k in range(1, cols):
            s = s + ref[k].astype(F32)
        return s

    waits(sA, rA, semA)
    mine = walk(total(rA)) - SUB
    subs[0] = mine.astype(F32)

    def stepS(k, _):
        to_cols(subs.at[0], subs.at[k], semS, k).start()
        return 0

    lax.fori_loop(1, cols, stepS, 0)

    def deep_bits(c, sub):
        sub = jnp.broadcast_to(sub, (SUB, C)).astype(BF16)
        got = jnp.zeros((SUB, C), BF16)
        for t in range(16):
            got = got + jnp.where(sub == BF16(t), tab[t * SUB : (t + 1) * SUB, chunk(c)], BF16(0))
        return jnp.where(got.astype(F32) > 0.0, 1.0, 0.0).astype(BF16)

    def stepB(k, _):
        to_cols(subs.at[0], subs.at[k], semS, k).wait_recv()
        back = cols - k
        sB[back] = deep_bits(col_of(back), subs[k])
        to_cols(sB.at[back], rB.at[back], semB, back).start()
        return 0

    lax.fori_loop(1, cols, stepB, 0)
    rB[0] = deep_bits(me, subs[0])
    leaf = leaf_ref[...]
    high = leaf.astype(BF16).astype(F32)
    mid = (leaf - high).astype(BF16).astype(F32)
    low = leaf - high - mid
    r16 = lax.broadcasted_iota(jnp.int32, (16, 256), 0)
    leaves = jnp.where(r16 == 0, high, jnp.where(r16 == 1, mid, jnp.where(r16 == 2, low, 0.0))).astype(BF16)
    waits(sB, rB, semB)
    at = mine * 16 + walk(total(rB)) - SUB
    onehot = jnp.where(lax.broadcasted_iota(jnp.int32, (256, C), 0) == at, 1.0, 0.0).astype(BF16)
    parts = jnp.dot(leaves, onehot, preferred_element_type=F32)
    weight = parts[0:1] + parts[1:2] + parts[2:3]
    ps[0] = jax.nn.sigmoid(base_ref[me] + weight)

    def stepP(k, _):
        to_cols(ps.at[0], ps.at[k], semP, k).start()
        return 0

    lax.fori_loop(1, cols, stepP, 0)

    def weights(k, c):
        p = ps[k]
        gradient = (p - labels_ref[c].astype(F32)).astype(BF16).astype(F32)
        hessian = (p * (1.0 - p)).astype(BF16).astype(F32) * 4.0
        node = jnp.broadcast_to(node_ref[c], (NODES, C)) == lax.broadcasted_iota(jnp.int32, (NODES, C), 0)
        for i, (a, b) in enumerate(zip(pieces_of(gradient), pieces_of(hessian))):
            both = jnp.concatenate([jnp.where(node, a, 0.0), jnp.where(node, b, 0.0)], axis=0)
            W[i * 32 : (i + 1) * 32, chunk(c)] = both.astype(F8)

    weights(0, me)

    def stepW(k, _):
        to_cols(ps.at[0], ps.at[k], semP, k).wait_recv()
        weights(k, col_of(cols - k))
        return 0

    lax.fori_loop(1, cols, stepW, 0)

    def pair(k):
        return pltpu.make_async_remote_copy(
            src_ref=pair_s.at[k], dst_ref=pair_r.at[k], send_sem=semX.at[0, k], recv_sem=semX.at[1, k],
            device_id=(chip * 2 + 1 - core, me), device_id_type=MESH,
        )

    def share(k):
        return pltpu.make_async_remote_copy(
            src_ref=hs.at[k], dst_ref=hr.at[k], send_sem=semH.at[0, k], recv_sem=semH.at[1, k],
            device_id=(chip_of(k) * 2 + core, me), device_id_type=MESH,
        )

    halves = 2
    Kc = samples // halves
    bins = lax.broadcasted_iota(jnp.int32, (BINS, Kc), 0).astype(I8)

    def block(k):
        g = chip_of(k)
        acc = jnp.zeros((32 * PIECES, GROUP * BINS), F32)
        for s in range(halves):
            at = slice(s * Kc, (s + 1) * Kc)
            onehot = jnp.concatenate(
                [
                    jnp.where(jnp.broadcast_to(cs[g, f : f + 1, at], (BINS, Kc)) == bins, jnp.ones((), F8), jnp.zeros((), F8))
                    for f in range(GROUP)
                ],
                axis=0,
            )
            acc = acc + lax.dot_general(W[:, at], onehot, (((1,), (1,)), ((), ())), preferred_element_type=F32)
        out = acc[0:32] * PIECE_SCALES[0]
        for i in range(1, PIECES):
            out = out + acc[i * 32 : (i + 1) * 32] * PIECE_SCALES[i]
        out = jnp.concatenate([out[0:16], out[16:32] * 0.25], axis=0)
        left, right = out[:, 0:128], out[:, 128:256]
        first = core == 0
        hs[k] = jnp.where(first, left, right)
        pair_s[k] = jnp.where(first, right, left)
        pair(k).start()

    def merge(k):
        pair(k).wait_recv()
        hs[k] = hs[k] + pair_r[k]

    def stepH(i, _):
        block(i)

        @pl.when(i > 1)
        def _():
            merge(i - 1)
            share(i - 1).start()

        return 0

    lax.fori_loop(1, chips, stepH, 0)
    block(0)
    merge(chips - 1)
    share(chips - 1).start()
    merge(0)
    hist = hs[0]

    def stepR(k, h):
        share(k).wait_recv()
        return h + hr[k]

    hist = lax.fori_loop(1, chips, stepR, hist)

    i0 = lax.broadcasted_iota(jnp.int32, (128, 128), 0)
    i1 = lax.broadcasted_iota(jnp.int32, (128, 128), 1)
    same = (i0 // BINS) == (i1 // BINS)
    upto = jnp.where(same & (i0 <= i1), 1.0, 0.0)
    whole = jnp.where(same, 1.0, 0.0)
    left = jnp.dot(hist, upto, precision=lax.Precision.HIGHEST, preferred_element_type=F32)
    node = jnp.dot(hist, whole, precision=lax.Precision.HIGHEST, preferred_element_type=F32)
    right = node - left

    def score(s):
        return s[0:16] * s[0:16] / (s[16:32] + reg_lambda)

    gains = 0.5 * (score(left) + score(right) - score(node))
    gains_ref[...] = gains

    best = jnp.max(gains, axis=1, keepdims=True)
    d0 = lax.broadcasted_iota(jnp.int32, (16, 128), 0)
    d1 = lax.broadcasted_iota(jnp.int32, (16, 128), 1)
    best = jnp.max(jnp.where(d0 == d1, best, -jnp.inf), axis=0, keepdims=True)
    m1s[...] = best

    def first(k):
        return pltpu.make_async_remote_copy(
            src_ref=m1s, dst_ref=m1r.at[k], send_sem=semM.at[0, k], recv_sem=semM.at[1, k],
            device_id=(chip_of(k) * 2 + core, me), device_id_type=MESH,
        )

    def second(k):
        other, c = k // cols, lax.rem(k, cols)
        return pltpu.make_async_remote_copy(
            src_ref=m2s, dst_ref=m2r.at[k], send_sem=semN.at[0, k], recv_sem=semN.at[1, k],
            device_id=(chip * 2 + lax.rem(core + other, 2), col_of(c)), device_id_type=MESH,
        )

    def exchange(n, copy, got, best):
        def go(k, _):
            copy(k).start()
            return 0

        def take(k, b):
            copy(k).wait_recv()
            return jnp.maximum(b, got[k])

        lax.fori_loop(1, n, go, 0)
        return lax.fori_loop(1, n, take, best)

    best = exchange(chips, first, m1r, best)
    m2s[...] = best
    best = exchange(2 * cols, second, m2r, best)
    best_ref[...] = best[:, 0:16]

    sends(sA, rA, semA)
    sends(sB, rB, semB)

    def leftS(k, _):
        to_cols(subs.at[0], subs.at[k], semS, k).wait_send()
        to_cols(ps.at[0], ps.at[k], semP, k).wait_send()
        return 0

    lax.fori_loop(1, cols, leftS, 0)

    def leftX(k, _):
        pair(k).wait_send()
        return 0

    lax.fori_loop(0, chips, leftX, 0)

    def leftH(k, _):
        share(k).wait_send()
        first(k).wait_send()
        return 0

    lax.fori_loop(1, chips, leftH, 0)

    def leftN(k, _):
        second(k).wait_send()
        return 0

    lax.fori_loop(1, 2 * cols, leftN, 0)


def by_subtree(slots):
    parts = [slots[0:16].reshape(16, 1)]
    for level in range(4):
        n = 2**level
        parts.append(slots[16 * n : 32 * n].reshape(16, n))
    return jnp.concatenate(parts, axis=1).reshape(1, 256)


def shards(cols, rows, codes, labels, base_margin, node_id, split_feature, threshold, leaf_value):
    feats, samples = codes.shape
    chips = rows // 2
    C = samples // cols
    vm = pl.BlockSpec(memory_space=pltpu.VMEM)
    dma = pltpu.SemaphoreType.DMA
    by_col = lambda a: a.reshape(cols, 1, C)
    gains, best = pl.pallas_call(
        functools.partial(kernel, cols, chips),
        out_shape=(jax.ShapeDtypeStruct((NODES, 128), F32), jax.ShapeDtypeStruct((1, NODES), F32)),
        in_specs=[vm] * 9,
        out_specs=(vm, vm),
        scratch_shapes=[
            pltpu.VMEM((feats + 16, samples), BF16),
            pltpu.VMEM((chips, GROUP, samples), I8),
            pltpu.VMEM((256, samples), BF16),
            pltpu.VMEM((cols, SUB, C), BF16),
            pltpu.VMEM((cols, SUB, C), BF16),
            pltpu.VMEM((cols, SUB, C), BF16),
            pltpu.VMEM((cols, SUB, C), BF16),
            pltpu.VMEM((cols, 1, C), F32),
            pltpu.VMEM((cols, 1, C), F32),
            pltpu.VMEM((32 * PIECES, samples), F8),
            pltpu.VMEM((chips, 32, 128), F32),
            pltpu.VMEM((chips, 32, 128), F32),
            pltpu.VMEM((chips, 32, 128), F32),
            pltpu.VMEM((chips, 32, 128), F32),
            pltpu.VMEM((1, 128), F32),
            pltpu.VMEM((chips, 1, 128), F32),
            pltpu.VMEM((1, 128), F32),
            pltpu.VMEM((2 * cols, 1, 128), F32),
            dma((2, cols)),
            dma((2, cols)),
            dma((2, cols)),
            dma((2, cols)),
            dma((2, chips)),
            dma((2, chips)),
            dma((2, chips)),
            dma((2, 2 * cols)),
        ],
        compiler_params=pltpu.CompilerParams(
            collective_id=0, has_side_effects=True, vmem_limit_bytes=56 * 2**20
        ),
        cost_estimate=pl.CostEstimate(flops=2 * 256 * samples * feats * BINS, bytes_accessed=4 * feats * samples, transcendentals=samples),
    )(
        codes, by_col(labels), by_col(base_margin), by_col(node_id),
        split_feature.reshape(1, 256), threshold.reshape(1, 256),
        by_subtree(split_feature), by_subtree(threshold), leaf_value.reshape(1, 256),
    )
    return gains, best.reshape(NODES)


def solution(mesh):
    return jax.shard_map(
        functools.partial(shards, mesh.shape["cols"], mesh.shape["rows"]),
        mesh=mesh,
        in_specs=(P("cols", "rows"), P("rows"), P("rows"), P("rows"), P(), P(), P()),
        out_specs=(P(None, ("cols", "rows")), P()),
        check_vma=False,
    )
```

```python
import functools

import jax
import jax.numpy as jnp
from jax import lax
from jax.experimental import pallas as pl
from jax.experimental.pallas import tpu as pltpu
from jax.sharding import PartitionSpec as P

BINS = 64
NODES = 16
SUB = 16
PIECES = 8
GROUP = 4
PARTS = 2
reg_lambda = 1.0
MESH = pl.DeviceIdType.MESH
F32, BF16, F8, I8 = jnp.float32, jnp.bfloat16, jnp.float8_e4m3fn, jnp.int8
PIECE_SCALES = [4.0**i / 2048.0 for i in range(6)] + [2.0**-19, 2.0**-23]


def walk(bits):
    rows = lax.broadcasted_iota(jnp.int32, bits.shape, 0)
    slot = jnp.ones((1, bits.shape[1]), jnp.int32)
    for _ in range(4):
        bit = jnp.sum(jnp.where(rows == slot, bits, 0.0), axis=0, keepdims=True)
        slot = 2 * slot + bit.astype(jnp.int32)
    return slot


def pieces_of(value):
    scaled = value * 2048.0
    whole = jnp.floor(scaled + 0.5)
    rest = (scaled - whole) * 256.0
    digits = []
    for _ in range(5):
        upper = jnp.floor(whole * 0.25 + 0.5)
        digits.append(whole - 4.0 * upper)
        whole = upper
    digits.append(whole)
    wide = rest * 1048577.0
    top = wide - (wide - rest)
    return digits + [top, (rest - top) * 16.0]


def wait_bytes(ref, sem):
    pltpu.make_async_copy(ref, ref, sem).wait()


def kernel(
    cols, chips,
    codes_in, labels_in, base_in, node_in, sf_in, thr_in, leaf_in,
    out_ref,
    codes_ref, labels_ref, base_ref, node_ref, sf_ref, thr_ref, leaf_ref, sums,
    aug, cs, tab, sA, rA, sB, rB, subs, ps, W, pair_s, pair_r, hs, hr, m1s, m1r, m2s, m2r,
    semA, semS, semB, semP, sentS, sentP, semX, sentX, semH, semM, semN, semC, semI,
):
    feats, samples = codes_ref.shape
    Kc = samples // PARTS
    C = Kc // cols
    me = lax.axis_index("cols")
    row = lax.axis_index("rows")
    chip, core = row // 2, lax.rem(row, 2)
    planes = 2
    ring = chips // planes
    plane, place = chip // ring, lax.rem(chip, ring)

    def col_of(k):
        return lax.rem(me + k, cols)

    def chunk(q, c):
        return pl.ds(pl.multiple_of((q * cols + c) * C, C), C)

    barrier = pltpu.get_barrier_semaphore()

    def greet(r, c):
        pl.semaphore_signal(barrier, inc=1, device_id=(r, c), device_id_type=MESH)

    for k in range(1, chips):
        greet(lax.rem(chip + k, chips) * 2 + core, me)
    for k in range(1, cols):
        greet(row, col_of(k))
    for k in range(cols):
        greet(chip * 2 + 1 - core, col_of(k))

    small = [
        pltpu.make_async_copy(a, b, semI.at[n])
        for n, (a, b) in enumerate(
            [(sf_in, sf_ref), (thr_in, thr_ref), (leaf_in, leaf_ref), (base_in, base_ref), (labels_in, labels_ref), (node_in, node_ref)]
        )
    ]
    big = []
    for q in range(PARTS):
        at = pl.ds(q * Kc, Kc)
        big.append(pltpu.make_async_copy(codes_in.at[:, at], codes_ref.at[:, at], semC.at[q]))
    for copy in small[:2] + big + small[2:]:
        copy.start()

    i0 = lax.broadcasted_iota(jnp.int32, (128, 256), 0)
    i1 = lax.broadcasted_iota(jnp.int32, (128, 256), 1)
    same = (i0 // BINS) == ((i1 % 128) // BINS)
    sums[...] = jnp.where(same & ((i0 <= i1) | (i1 >= 128)), 1.0, 0.0)

    aug[feats:, :] = jnp.where(lax.broadcasted_iota(jnp.int32, (16, samples), 0) == 0, 1.0, 0.0).astype(BF16)

    for copy in small[:2]:
        copy.wait()

    ids = lax.broadcasted_iota(jnp.int32, (feats, 256), 0) + me * feats
    low = lax.broadcasted_iota(jnp.int32, (16, 256), 0) == 0
    picks = jnp.concatenate(
        [jnp.where(sf_ref[...] == ids, 1.0, 0.0), jnp.where(low, -thr_ref[...].astype(F32), 0.0)], axis=0
    ).astype(BF16)

    def rows_of(slots):
        order = jnp.where(slots == lax.broadcasted_iota(jnp.int32, slots.shape, 1), 1.0, 0.0).astype(BF16)
        return lax.dot_general(order, picks, (((1,), (1,)), ((), ())), preferred_element_type=F32).astype(BF16)

    top = rows_of(lax.broadcasted_iota(jnp.int32, (SUB, 256), 0))

    for q in range(PARTS):
        at = slice(q * Kc, (q + 1) * Kc)
        big[q].wait()
        aug[0:feats, at] = codes_ref[:, at].astype(BF16)

    pl.semaphore_wait(barrier, (cols - 1) + cols + (chips - 1))

    def to_col(src, dst, sent, came, k):
        return pltpu.make_async_remote_copy(
            src_ref=src, dst_ref=dst, send_sem=sent, recv_sem=came, device_id=(row, col_of(k)), device_id_type=MESH
        )

    others = pl.ds(1, cols - 1)

    def top_bits(q, c):
        t = jnp.dot(top, aug[:, chunk(q, c)], preferred_element_type=F32)
        return jnp.where(t > 0.0, 1.0, 0.0).astype(BF16)

    for q in range(PARTS):
        for k in range(1, cols):
            sA[q, k] = top_bits(q, col_of(k))
            to_col(sA.at[q, k], rA.at[q, k], semA.at[0, q], semA.at[1, q], k).start()
        rA[q, 0] = top_bits(q, me)

    at = lax.broadcasted_iota(jnp.int32, (256, 256), 0)
    t, r = at // SUB, at % SUB
    width = jnp.where(r >= 8, 8, jnp.where(r >= 4, 4, jnp.where(r >= 2, 2, 1)))
    deep = rows_of((16 + t) * width + r - width)

    def table(n, _):
        where = pl.ds(pl.multiple_of(n * C, C), C)
        tab[:, where] = jnp.dot(deep, aug[:, where], preferred_element_type=F32).astype(BF16)
        return 0

    lax.fori_loop(0, PARTS * cols, table, 0)

    def total(ref, q):
        s = ref[q, 0].astype(F32)
        for k in range(1, cols):
            s = s + ref[q, k].astype(F32)
        return s

    mine = []
    for q in range(PARTS):
        wait_bytes(rA.at[q, others], semA.at[1, q])
        mine.append(walk(total(rA, q)) - SUB)
        subs[q, 0] = mine[q].astype(F32)
        for k in range(1, cols):
            to_col(subs.at[q, 0], subs.at[q, k], sentS.at[q], semS.at[q, k], k).start()

    def deep_bits(q, c, sub):
        sub = jnp.broadcast_to(sub, (SUB, C)).astype(BF16)
        got = jnp.zeros((SUB, C), BF16)
        for t in range(16):
            got = got + jnp.where(sub == BF16(t), tab[t * SUB : (t + 1) * SUB, chunk(q, c)], BF16(0))
        return jnp.where(got.astype(F32) > 0.0, 1.0, 0.0).astype(BF16)

    for q in range(PARTS):
        rB[q, 0] = deep_bits(q, me, mine[q].astype(F32))

        def stepB(k, _):
            wait_bytes(subs.at[q, k], semS.at[q, k])
            back = cols - k
            sB[q, back] = deep_bits(q, col_of(back), subs[q, k])
            to_col(sB.at[q, back], rB.at[q, back], semB.at[0, q], semB.at[1, q], back).start()
            return 0

        lax.fori_loop(1, cols, stepB, 0)

    for copy in small[2:]:
        copy.wait()
    leaf = leaf_ref[...]
    high = leaf.astype(BF16).astype(F32)
    mid = (leaf - high).astype(BF16).astype(F32)
    rest = leaf - high - mid
    r16 = lax.broadcasted_iota(jnp.int32, (16, 256), 0)
    leaves = jnp.where(r16 == 0, high, jnp.where(r16 == 1, mid, jnp.where(r16 == 2, rest, 0.0))).astype(BF16)

    v8 = codes_ref[...].astype(I8)
    for g in range(chips):
        cs[g] = v8[GROUP * g : GROUP * (g + 1)]

    for q in range(PARTS):
        wait_bytes(rB.at[q, others], semB.at[1, q])
        slot = mine[q] * 16 + walk(total(rB, q)) - SUB
        onehot = jnp.where(lax.broadcasted_iota(jnp.int32, (256, C), 0) == slot, 1.0, 0.0).astype(BF16)
        parts = jnp.dot(leaves, onehot, preferred_element_type=F32)
        weight = parts[0:1] + parts[1:2] + parts[2:3]
        ps[q, 0] = jax.nn.sigmoid(base_ref[q * cols + me] + weight)
        for k in range(1, cols):
            to_col(ps.at[q, 0], ps.at[q, k], sentP.at[q], semP.at[q, k], k).start()

    def weights(q, k, c):
        p = ps[q, k]
        n = q * cols + c
        gradient = (p - labels_ref[n].astype(F32)).astype(BF16).astype(F32)
        hessian = (p * (1.0 - p)).astype(BF16).astype(F32) * 4.0
        here = jnp.broadcast_to(node_ref[n].astype(F32), (NODES, C)).astype(BF16)
        node = here == lax.broadcasted_iota(jnp.int32, (NODES, C), 0).astype(F32).astype(BF16)
        for i, v in enumerate(pieces_of(jnp.concatenate([gradient, hessian], axis=0))):
            a = jnp.broadcast_to(v[0:1], (NODES, C)).astype(BF16)
            b = jnp.broadcast_to(v[1:2], (NODES, C)).astype(BF16)
            both = jnp.concatenate([jnp.where(node, a, BF16(0)), jnp.where(node, b, BF16(0))], axis=0)
            W[i * 32 : (i + 1) * 32, chunk(q, c)] = both.astype(F8)

    def all_weights(q):
        weights(q, 0, me)

        def stepW(k, _):
            wait_bytes(ps.at[q, k], semP.at[q, k])
            weights(q, k, col_of(cols - k))
            return 0

        lax.fori_loop(1, cols, stepW, 0)

    def chip_of(i):
        j, far = lax.rem(i, ring), 1 - i // ring
        odd = lax.rem(j, 2)
        dz = odd * (ring // 2 - (j + 1) // 2) + (1 - odd) * (ring // 2 + j // 2)
        return lax.rem(plane + far, planes) * ring + lax.rem(place + dz, ring)

    def pair(i):
        return pltpu.make_async_remote_copy(
            src_ref=pair_s.at[i], dst_ref=pair_r.at[i], send_sem=sentX.at[0], recv_sem=semX.at[i],
            device_id=(chip * 2 + 1 - core, me), device_id_type=MESH,
        )

    def share(i):
        return pltpu.make_async_remote_copy(
            src_ref=hs.at[i], dst_ref=hr.at[i], send_sem=semH.at[0], recv_sem=semH.at[1],
            device_id=(chip_of(i) * 2 + core, me), device_id_type=MESH,
        )

    for q in range(PARTS):
        all_weights(q)

    bins = lax.broadcasted_iota(jnp.int32, (BINS, samples), 0).astype(I8)

    def block(i):
        g = chip_of(i)
        onehot = jnp.concatenate(
            [
                jnp.where(
                    jnp.broadcast_to(cs[g, f : f + 1, :], (BINS, samples)) == bins, jnp.ones((), F8), jnp.zeros((), F8)
                )
                for f in range(GROUP)
            ],
            axis=0,
        )
        acc = lax.dot_general(W[...], onehot, (((1,), (1,)), ((), ())), preferred_element_type=F32)
        out = acc[0:32] * PIECE_SCALES[0]
        for n in range(1, PIECES):
            out = out + acc[n * 32 : (n + 1) * 32] * PIECE_SCALES[n]
        out = jnp.concatenate([out[0:16], out[16:32] * 0.25], axis=0)
        left, right = out[:, 0:128], out[:, 128:256]
        first = core == 0
        hs[i] = jnp.where(first, left, right)
        pair_s[i] = jnp.where(first, right, left)
        pair(i).start()

    def merge(i):
        wait_bytes(pair_r.at[i], semX.at[i])
        hs[i] = hs[i] + pair_r[i]

    def stepH(n, _):
        block(2 * n)

        @pl.when(n > 0)
        def _():
            merge(2 * n - 1)
            share(2 * n - 1).start()

        block(2 * n + 1)
        merge(2 * n)
        share(2 * n).start()
        return 0

    lax.fori_loop(0, chips // 2, stepH, 0)
    merge(chips - 1)
    wait_bytes(hr.at[pl.ds(0, chips - 1)], semH.at[1])
    hist = hs[chips - 1]
    for i in range(chips - 1):
        hist = hist + hr[i]

    both = jnp.dot(hist, sums[...], precision=lax.Precision.HIGHEST, preferred_element_type=F32)
    left, node = both[:, 0:128], both[:, 128:256]
    right = node - left

    def score(s):
        return s[0:16] * s[0:16] / (s[16:32] + reg_lambda)

    gains = 0.5 * (score(left) + score(right) - score(node))
    out_ref[0:NODES, :] = gains

    best = jnp.max(gains, axis=1, keepdims=True)
    d0 = lax.broadcasted_iota(jnp.int32, (16, 128), 0)
    d1 = lax.broadcasted_iota(jnp.int32, (16, 128), 1)
    best = jnp.max(jnp.where(d0 == d1, best, -jnp.inf), axis=0, keepdims=True)

    def exchange(n, src, got, sem, device, best):
        src[...] = best
        for k in range(1, n):
            pltpu.make_async_remote_copy(
                src_ref=src, dst_ref=got.at[k], send_sem=sem.at[0], recv_sem=sem.at[1],
                device_id=device(k), device_id_type=MESH,
            ).start()
        wait_bytes(got.at[pl.ds(1, n - 1)], sem.at[1])
        for k in range(1, n):
            best = jnp.maximum(best, got[k])
        return best

    best = exchange(chips, m1s, m1r, semM, lambda k: (lax.rem(chip + k, chips) * 2 + core, me), best)
    best = exchange(
        2 * cols, m2s, m2r, semN, lambda k: (chip * 2 + lax.rem(core + k // cols, 2), col_of(k % cols)), best
    )
    out_ref[NODES:, :] = jnp.broadcast_to(best, (8, 128))

    for q in range(PARTS):
        wait_bytes(sA.at[q, others], semA.at[0, q])
        wait_bytes(sB.at[q, others], semB.at[0, q])
        wait_bytes(subs.at[q, others], sentS.at[q])
        wait_bytes(ps.at[q, others], sentP.at[q])
    wait_bytes(pair_s, sentX.at[0])
    wait_bytes(hs.at[pl.ds(0, chips - 1)], semH.at[0])
    wait_bytes(m1r.at[pl.ds(1, chips - 1)], semM.at[0])
    wait_bytes(m2r.at[pl.ds(1, 2 * cols - 1)], semN.at[0])


def shards(cols, rows, codes, labels, base_margin, node_id, split_feature, threshold, leaf_value):
    feats, samples = codes.shape
    chips = rows // 2
    C = samples // (cols * PARTS)
    vm = pl.BlockSpec(memory_space=pltpu.VMEM)
    anywhere = pl.BlockSpec(memory_space=pl.ANY)
    I32 = jnp.int32
    dma = pltpu.SemaphoreType.DMA
    by_chunk = lambda a: a.reshape(cols * PARTS, 1, C)
    out = pl.pallas_call(
        functools.partial(kernel, cols, chips),
        out_shape=jax.ShapeDtypeStruct((NODES + 8, 128), F32),
        in_specs=[anywhere] * 7,
        out_specs=vm,
        scratch_shapes=[
            pltpu.VMEM((feats, samples), I32),
            pltpu.VMEM((cols * PARTS, 1, C), I32),
            pltpu.VMEM((cols * PARTS, 1, C), F32),
            pltpu.VMEM((cols * PARTS, 1, C), I32),
            pltpu.VMEM((1, 256), I32),
            pltpu.VMEM((1, 256), I32),
            pltpu.VMEM((1, 256), F32),
            pltpu.VMEM((128, 256), F32),
            pltpu.VMEM((feats + 16, samples), BF16),
            pltpu.VMEM((chips, GROUP, samples), I8),
            pltpu.VMEM((256, samples), BF16),
            pltpu.VMEM((PARTS, cols, SUB, C), BF16),
            pltpu.VMEM((PARTS, cols, SUB, C), BF16),
            pltpu.VMEM((PARTS, cols, SUB, C), BF16),
            pltpu.VMEM((PARTS, cols, SUB, C), BF16),
            pltpu.VMEM((PARTS, cols, 1, C), F32),
            pltpu.VMEM((PARTS, cols, 1, C), F32),
            pltpu.VMEM((32 * PIECES, samples), F8),
            pltpu.VMEM((chips, 32, 128), F32),
            pltpu.VMEM((chips, 32, 128), F32),
            pltpu.VMEM((chips, 32, 128), F32),
            pltpu.VMEM((chips, 32, 128), F32),
            pltpu.VMEM((1, 128), F32),
            pltpu.VMEM((chips, 1, 128), F32),
            pltpu.VMEM((1, 128), F32),
            pltpu.VMEM((2 * cols, 1, 128), F32),
            dma((2, PARTS)),
            dma((PARTS, cols)),
            dma((2, PARTS)),
            dma((PARTS, cols)),
            dma((PARTS,)),
            dma((PARTS,)),
            dma((chips,)),
            dma((1,)),
            dma((2,)),
            dma((2,)),
            dma((2,)),
            dma((PARTS,)),
            dma((6,)),
        ],
        compiler_params=pltpu.CompilerParams(
            collective_id=0, has_side_effects=True, vmem_limit_bytes=56 * 2**20
        ),
        cost_estimate=pl.CostEstimate(
            flops=2 * 256 * samples * feats * BINS, bytes_accessed=4 * feats * samples, transcendentals=samples
        ),
    )(
        codes, by_chunk(labels), by_chunk(base_margin), by_chunk(node_id),
        split_feature.reshape(1, 256), threshold.reshape(1, 256), leaf_value.reshape(1, 256),
    )
    return out[0:NODES], out[NODES, 0:NODES]


def solution(mesh):
    return jax.shard_map(
        functools.partial(shards, mesh.shape["cols"], mesh.shape["rows"]),
        mesh=mesh,
        in_specs=(P("cols", "rows"), P("rows"), P("rows"), P("rows"), P(), P(), P()),
        out_specs=(P(None, ("cols", "rows")), P()),
        check_vma=False,
    )
```

```python
import functools

import jax
import jax.numpy as jnp
from jax import lax
from jax.experimental import pallas as pl
from jax.experimental.pallas import tpu as pltpu
from jax.sharding import PartitionSpec as P

BINS = 64
NODES = 16
SUB = 16
PIECES = 8
GROUP = 4
PARTS = 2
reg_lambda = 1.0
MESH = pl.DeviceIdType.MESH
F32, BF16, F8, I8 = jnp.float32, jnp.bfloat16, jnp.float8_e4m3fn, jnp.int8
PIECE_SCALES = [4.0**i / 2048.0 for i in range(6)] + [2.0**-19, 2.0**-23]


def walk(bits):
    rows = lax.broadcasted_iota(jnp.int32, bits.shape, 0)
    slot = jnp.ones((1, bits.shape[1]), jnp.int32)
    for _ in range(4):
        bit = jnp.sum(jnp.where(rows == slot, bits, 0.0), axis=0, keepdims=True)
        slot = 2 * slot + bit.astype(jnp.int32)
    return slot


def pieces_of(value):
    scaled = value * 2048.0
    whole = jnp.floor(scaled + 0.5)
    rest = (scaled - whole) * 256.0
    digits = []
    for _ in range(5):
        upper = jnp.floor(whole * 0.25 + 0.5)
        digits.append(whole - 4.0 * upper)
        whole = upper
    digits.append(whole)
    wide = rest * 1048577.0
    top = wide - (wide - rest)
    return digits + [top, (rest - top) * 16.0]


def wait_bytes(ref, sem):
    pltpu.make_async_copy(ref, ref, sem).wait()


def kernel(
    cols, chips,
    codes_in, labels_in, base_in, node_in, sf_in, thr_in, leaf_in,
    out_ref,
    codes_ref, labels_ref, base_ref, node_ref, sf_ref, thr_ref, leaf_ref, sums,
    aug, cs, tab, sA, rA, sB, rB, subs, ps, W, pair_s, pair_r, hs, hr, m1s, m1r, m2s, m2r,
    semA, semS, semB, semP, sentS, sentP, semX, sentX, semH, semM, semN, semC, semI,
):
    feats, samples = codes_ref.shape
    Kc = samples // PARTS
    C = Kc // cols
    me = lax.axis_index("cols")
    row = lax.axis_index("rows")
    chip, core = row // 2, lax.rem(row, 2)
    planes = 2
    ring = chips // planes
    plane, place = chip // ring, lax.rem(chip, ring)

    def col_of(k):
        return lax.rem(me + k, cols)

    def chunk(q, c):
        return pl.ds(pl.multiple_of((q * cols + c) * C, C), C)

    barrier = pltpu.get_barrier_semaphore()

    def greet(r, c):
        pl.semaphore_signal(barrier, inc=1, device_id=(r, c), device_id_type=MESH)

    for k in range(1, chips):
        greet(lax.rem(chip + k, chips) * 2 + core, me)
    for k in range(1, cols):
        greet(row, col_of(k))
    for k in range(cols):
        greet(chip * 2 + 1 - core, col_of(k))

    small = [
        pltpu.make_async_copy(a, b, semI.at[n])
        for n, (a, b) in enumerate(
            [(sf_in, sf_ref), (thr_in, thr_ref), (leaf_in, leaf_ref), (base_in, base_ref), (labels_in, labels_ref), (node_in, node_ref)]
        )
    ]
    big = []
    for q in range(PARTS):
        at = pl.ds(q * Kc, Kc)
        big.append(pltpu.make_async_copy(codes_in.at[:, at], codes_ref.at[:, at], semC.at[q]))
    for copy in small[:2] + big + small[2:]:
        copy.start()

    i0 = lax.broadcasted_iota(jnp.int32, (128, 256), 0)
    i1 = lax.broadcasted_iota(jnp.int32, (128, 256), 1)
    same = (i0 // BINS) == ((i1 % 128) // BINS)
    sums[...] = jnp.where(same & ((i0 <= i1) | (i1 >= 128)), 1.0, 0.0)

    aug[feats:, :] = jnp.where(lax.broadcasted_iota(jnp.int32, (16, samples), 0) == 0, 1.0, 0.0).astype(BF16)

    for copy in small[:2]:
        copy.wait()

    ids = lax.broadcasted_iota(jnp.int32, (feats, 256), 0) + me * feats
    low = lax.broadcasted_iota(jnp.int32, (16, 256), 0) == 0
    picks = jnp.concatenate(
        [jnp.where(sf_ref[...] == ids, 1.0, 0.0), jnp.where(low, -thr_ref[...].astype(F32), 0.0)], axis=0
    ).astype(BF16)

    def rows_of(slots):
        order = jnp.where(slots == lax.broadcasted_iota(jnp.int32, slots.shape, 1), 1.0, 0.0).astype(BF16)
        return lax.dot_general(order, picks, (((1,), (1,)), ((), ())), preferred_element_type=F32).astype(BF16)

    top = rows_of(lax.broadcasted_iota(jnp.int32, (SUB, 256), 0))

    for q in range(PARTS):
        at = slice(q * Kc, (q + 1) * Kc)
        big[q].wait()
        aug[0:feats, at] = codes_ref[:, at].astype(BF16)

    pl.semaphore_wait(barrier, (cols - 1) + cols + (chips - 1))

    def to_col(src, dst, sent, came, k):
        return pltpu.make_async_remote_copy(
            src_ref=src, dst_ref=dst, send_sem=sent, recv_sem=came, device_id=(row, col_of(k)), device_id_type=MESH
        )

    others = pl.ds(1, cols - 1)

    def top_bits(q, c):
        t = jnp.dot(top, aug[:, chunk(q, c)], preferred_element_type=F32)
        return jnp.where(t > 0.0, 1.0, 0.0).astype(BF16)

    for q in range(PARTS):
        for k in range(1, cols):
            sA[q, k] = top_bits(q, col_of(k))
            to_col(sA.at[q, k], rA.at[q, k], semA.at[0, q], semA.at[1, q], k).start()
        rA[q, 0] = top_bits(q, me)

    at = lax.broadcasted_iota(jnp.int32, (256, 256), 0)
    t, r = at // SUB, at % SUB
    width = jnp.where(r >= 8, 8, jnp.where(r >= 4, 4, jnp.where(r >= 2, 2, 1)))
    deep = rows_of((16 + t) * width + r - width)

    def table(n, _):
        where = pl.ds(pl.multiple_of(n * C, C), C)
        tab[:, where] = jnp.dot(deep, aug[:, where], preferred_element_type=F32).astype(BF16)
        return 0

    lax.fori_loop(0, PARTS * cols, table, 0)

    def total(ref, q):
        s = ref[q, 0].astype(F32)
        for k in range(1, cols):
            s = s + ref[q, k].astype(F32)
        return s

    mine = []
    for q in range(PARTS):
        wait_bytes(rA.at[q, others], semA.at[1, q])
        mine.append(walk(total(rA, q)) - SUB)
        subs[q, 0] = mine[q].astype(F32)
        for k in range(1, cols):
            to_col(subs.at[q, 0], subs.at[q, k], sentS.at[q], semS.at[q, k], k).start()

    def deep_bits(q, c, sub):
        sub = jnp.broadcast_to(sub, (SUB, C)).astype(BF16)
        got = jnp.zeros((SUB, C), BF16)
        for t in range(16):
            got = got + jnp.where(sub == BF16(t), tab[t * SUB : (t + 1) * SUB, chunk(q, c)], BF16(0))
        return jnp.where(got.astype(F32) > 0.0, 1.0, 0.0).astype(BF16)

    for q in range(PARTS):
        rB[q, 0] = deep_bits(q, me, mine[q].astype(F32))

        def stepB(k, _):
            wait_bytes(subs.at[q, k], semS.at[q, k])
            back = cols - k
            sB[q, back] = deep_bits(q, col_of(back), subs[q, k])
            to_col(sB.at[q, back], rB.at[q, back], semB.at[0, q], semB.at[1, q], back).start()
            return 0

        lax.fori_loop(1, cols, stepB, 0)

    for copy in small[2:]:
        copy.wait()
    leaf = leaf_ref[...]
    high = leaf.astype(BF16).astype(F32)
    mid = (leaf - high).astype(BF16).astype(F32)
    rest = leaf - high - mid
    r16 = lax.broadcasted_iota(jnp.int32, (16, 256), 0)
    leaves = jnp.where(r16 == 0, high, jnp.where(r16 == 1, mid, jnp.where(r16 == 2, rest, 0.0))).astype(BF16)

    v8 = codes_ref[...].astype(I8)
    for g in range(chips):
        cs[g] = v8[GROUP * g : GROUP * (g + 1)]

    for q in range(PARTS):
        wait_bytes(rB.at[q, others], semB.at[1, q])
        slot = mine[q] * 16 + walk(total(rB, q)) - SUB
        onehot = jnp.where(lax.broadcasted_iota(jnp.int32, (256, C), 0) == slot, 1.0, 0.0).astype(BF16)
        parts = jnp.dot(leaves, onehot, preferred_element_type=F32)
        weight = parts[0:1] + parts[1:2] + parts[2:3]
        ps[q, 0] = jax.nn.sigmoid(base_ref[q * cols + me] + weight)
        for k in range(1, cols):
            to_col(ps.at[q, 0], ps.at[q, k], sentP.at[q], semP.at[q, k], k).start()

    def weights(q, k, c):
        p = ps[q, k]
        n = q * cols + c
        gradient = (p - labels_ref[n].astype(F32)).astype(BF16).astype(F32)
        hessian = (p * (1.0 - p)).astype(BF16).astype(F32) * 4.0
        here = jnp.broadcast_to(node_ref[n].astype(F32), (NODES, C)).astype(BF16)
        node = here == lax.broadcasted_iota(jnp.int32, (NODES, C), 0).astype(F32).astype(BF16)
        for i, v in enumerate(pieces_of(jnp.concatenate([gradient, hessian], axis=0))):
            a = jnp.broadcast_to(v[0:1], (NODES, C)).astype(BF16)
            b = jnp.broadcast_to(v[1:2], (NODES, C)).astype(BF16)
            both = jnp.concatenate([jnp.where(node, a, BF16(0)), jnp.where(node, b, BF16(0))], axis=0)
            W[i * 32 : (i + 1) * 32, chunk(q, c)] = both.astype(F8)

    def all_weights(q):
        weights(q, 0, me)

        def stepW(k, _):
            wait_bytes(ps.at[q, k], semP.at[q, k])
            weights(q, k, col_of(cols - k))
            return 0

        lax.fori_loop(1, cols, stepW, 0)

    def chip_of(i):
        j, far = lax.rem(i, ring), 1 - i // ring
        odd = lax.rem(j, 2)
        dz = odd * (ring // 2 - (j + 1) // 2) + (1 - odd) * (ring // 2 + j // 2)
        return lax.rem(plane + far, planes) * ring + lax.rem(place + dz, ring)

    def pair(i):
        return pltpu.make_async_remote_copy(
            src_ref=pair_s.at[i], dst_ref=pair_r.at[i], send_sem=sentX.at[0], recv_sem=semX.at[i],
            device_id=(chip * 2 + 1 - core, me), device_id_type=MESH,
        )

    def share(i):
        return pltpu.make_async_remote_copy(
            src_ref=hs.at[i], dst_ref=hr.at[i], send_sem=semH.at[0], recv_sem=semH.at[1],
            device_id=(chip_of(i) * 2 + core, me), device_id_type=MESH,
        )

    for q in range(PARTS):
        all_weights(q)

    bins = lax.broadcasted_iota(jnp.int32, (BINS, samples), 0).astype(I8)

    def block(i):
        g = chip_of(i)
        onehot = jnp.concatenate(
            [
                jnp.where(
                    jnp.broadcast_to(cs[g, f : f + 1, :], (BINS, samples)) == bins, jnp.ones((), F8), jnp.zeros((), F8)
                )
                for f in range(GROUP)
            ],
            axis=0,
        )
        acc = lax.dot_general(W[...], onehot, (((1,), (1,)), ((), ())), preferred_element_type=F32)
        out = acc[0:32] * PIECE_SCALES[0]
        for n in range(1, PIECES):
            out = out + acc[n * 32 : (n + 1) * 32] * PIECE_SCALES[n]
        out = jnp.concatenate([out[0:16], out[16:32] * 0.25], axis=0)
        left, right = out[:, 0:128], out[:, 128:256]
        first = core == 0
        hs[i] = jnp.where(first, left, right)
        pair_s[i] = jnp.where(first, right, left)
        pair(i).start()

    def merge(i):
        wait_bytes(pair_r.at[i], semX.at[i])
        hs[i] = hs[i] + pair_r[i]

    def stepH(i, _):
        block(i)

        @pl.when(i > 0)
        def _():
            merge(i - 1)
            share(i - 1).start()

        return 0

    lax.fori_loop(0, chips, stepH, 0)
    merge(chips - 1)
    wait_bytes(hr.at[pl.ds(0, chips - 1)], semH.at[1])
    hist = hs[chips - 1]
    for i in range(chips - 1):
        hist = hist + hr[i]

    both = jnp.dot(hist, sums[...], precision=lax.Precision.HIGHEST, preferred_element_type=F32)
    left, node = both[:, 0:128], both[:, 128:256]
    right = node - left

    def score(s):
        return s[0:16] * s[0:16] / (s[16:32] + reg_lambda)

    gains = 0.5 * (score(left) + score(right) - score(node))
    out_ref[0:NODES, :] = gains

    best = jnp.max(gains, axis=1, keepdims=True)
    d0 = lax.broadcasted_iota(jnp.int32, (16, 128), 0)
    d1 = lax.broadcasted_iota(jnp.int32, (16, 128), 1)
    best = jnp.max(jnp.where(d0 == d1, best, -jnp.inf), axis=0, keepdims=True)

    def exchange(n, src, got, sem, device, best):
        src[...] = best
        for k in range(1, n):
            pltpu.make_async_remote_copy(
                src_ref=src, dst_ref=got.at[k], send_sem=sem.at[0], recv_sem=sem.at[1],
                device_id=device(k), device_id_type=MESH,
            ).start()
        wait_bytes(got.at[pl.ds(1, n - 1)], sem.at[1])
        for k in range(1, n):
            best = jnp.maximum(best, got[k])
        return best

    best = exchange(chips, m1s, m1r, semM, lambda k: (lax.rem(chip + k, chips) * 2 + core, me), best)
    best = exchange(
        2 * cols, m2s, m2r, semN, lambda k: (chip * 2 + lax.rem(core + k // cols, 2), col_of(k % cols)), best
    )
    out_ref[NODES:, :] = jnp.broadcast_to(best, (8, 128))

    for q in range(PARTS):
        wait_bytes(sA.at[q, others], semA.at[0, q])
        wait_bytes(sB.at[q, others], semB.at[0, q])
        wait_bytes(subs.at[q, others], sentS.at[q])
        wait_bytes(ps.at[q, others], sentP.at[q])
    wait_bytes(pair_s, sentX.at[0])
    wait_bytes(hs.at[pl.ds(0, chips - 1)], semH.at[0])
    wait_bytes(m1r.at[pl.ds(1, chips - 1)], semM.at[0])
    wait_bytes(m2r.at[pl.ds(1, 2 * cols - 1)], semN.at[0])


def shards(cols, rows, codes, labels, base_margin, node_id, split_feature, threshold, leaf_value):
    feats, samples = codes.shape
    chips = rows // 2
    C = samples // (cols * PARTS)
    vm = pl.BlockSpec(memory_space=pltpu.VMEM)
    anywhere = pl.BlockSpec(memory_space=pl.ANY)
    I32 = jnp.int32
    dma = pltpu.SemaphoreType.DMA
    by_chunk = lambda a: a.reshape(cols * PARTS, 1, C)
    out = pl.pallas_call(
        functools.partial(kernel, cols, chips),
        out_shape=jax.ShapeDtypeStruct((NODES + 8, 128), F32),
        in_specs=[anywhere] * 7,
        out_specs=vm,
        scratch_shapes=[
            pltpu.VMEM((feats, samples), I32),
            pltpu.VMEM((cols * PARTS, 1, C), I32),
            pltpu.VMEM((cols * PARTS, 1, C), F32),
            pltpu.VMEM((cols * PARTS, 1, C), I32),
            pltpu.VMEM((1, 256), I32),
            pltpu.VMEM((1, 256), I32),
            pltpu.VMEM((1, 256), F32),
            pltpu.VMEM((128, 256), F32),
            pltpu.VMEM((feats + 16, samples), BF16),
            pltpu.VMEM((chips, GROUP, samples), I8),
            pltpu.VMEM((256, samples), BF16),
            pltpu.VMEM((PARTS, cols, SUB, C), BF16),
            pltpu.VMEM((PARTS, cols, SUB, C), BF16),
            pltpu.VMEM((PARTS, cols, SUB, C), BF16),
            pltpu.VMEM((PARTS, cols, SUB, C), BF16),
            pltpu.VMEM((PARTS, cols, 1, C), F32),
            pltpu.VMEM((PARTS, cols, 1, C), F32),
            pltpu.VMEM((32 * PIECES, samples), F8),
            pltpu.VMEM((chips, 32, 128), F32),
            pltpu.VMEM((chips, 32, 128), F32),
            pltpu.VMEM((chips, 32, 128), F32),
            pltpu.VMEM((chips, 32, 128), F32),
            pltpu.VMEM((1, 128), F32),
            pltpu.VMEM((chips, 1, 128), F32),
            pltpu.VMEM((1, 128), F32),
            pltpu.VMEM((2 * cols, 1, 128), F32),
            dma((2, PARTS)),
            dma((PARTS, cols)),
            dma((2, PARTS)),
            dma((PARTS, cols)),
            dma((PARTS,)),
            dma((PARTS,)),
            dma((chips,)),
            dma((1,)),
            dma((2,)),
            dma((2,)),
            dma((2,)),
            dma((PARTS,)),
            dma((6,)),
        ],
        compiler_params=pltpu.CompilerParams(
            collective_id=0, has_side_effects=True, vmem_limit_bytes=56 * 2**20
        ),
        cost_estimate=pl.CostEstimate(
            flops=2 * 256 * samples * feats * BINS, bytes_accessed=4 * feats * samples, transcendentals=samples
        ),
    )(
        codes, by_chunk(labels), by_chunk(base_margin), by_chunk(node_id),
        split_feature.reshape(1, 256), threshold.reshape(1, 256), leaf_value.reshape(1, 256),
    )
    return out[0:NODES], out[NODES, 0:NODES]


def solution(mesh):
    return jax.shard_map(
        functools.partial(shards, mesh.shape["cols"], mesh.shape["rows"]),
        mesh=mesh,
        in_specs=(P("cols", "rows"), P("rows"), P("rows"), P("rows"), P(), P(), P()),
        out_specs=(P(None, ("cols", "rows")), P()),
        check_vma=False,
    )
```

```python
import functools

import jax
import jax.numpy as jnp
from jax import lax
from jax.experimental import pallas as pl
from jax.experimental.pallas import tpu as pltpu
from jax.sharding import PartitionSpec as P

BINS = 64
NODES = 16
SUB = 16
PIECES = 8
GROUP = 4
PARTS = 2
reg_lambda = 1.0
MESH = pl.DeviceIdType.MESH
F32, BF16, F8, I8 = jnp.float32, jnp.bfloat16, jnp.float8_e4m3fn, jnp.int8
PIECE_SCALES = [4.0**i / 2048.0 for i in range(6)] + [2.0**-19, 2.0**-23]


def walk(bits):
    rows = lax.broadcasted_iota(jnp.int32, bits.shape, 0)
    slot = jnp.ones((1, bits.shape[1]), jnp.int32)
    for _ in range(4):
        bit = jnp.sum(jnp.where(rows == slot, bits, 0.0), axis=0, keepdims=True)
        slot = 2 * slot + bit.astype(jnp.int32)
    return slot


def pieces_of(value):
    scaled = value * 2048.0
    whole = jnp.floor(scaled + 0.5)
    rest = (scaled - whole) * 256.0
    digits = []
    for _ in range(5):
        upper = jnp.floor(whole * 0.25 + 0.5)
        digits.append(whole - 4.0 * upper)
        whole = upper
    digits.append(whole)
    wide = rest * 1048577.0
    top = wide - (wide - rest)
    return digits + [top, (rest - top) * 16.0]


def wait_bytes(ref, sem):
    pltpu.make_async_copy(ref, ref, sem).wait()


def kernel(
    cols, chips,
    codes_in, labels_in, base_in, node_in, sf_in, thr_in, leaf_in,
    out_ref,
    codes_ref, labels_ref, base_ref, node_ref, sf_ref, thr_ref, leaf_ref, sums,
    aug, cs, tab, sA, rA, sB, rB, subs, ps, W, pair_s, pair_r, hs, hr, m1s, m1r, m2s, m2r,
    semA, semS, semB, semP, sentS, sentP, semX, sentX, semH, semM, semN, semC, semI,
):
    feats, samples = codes_ref.shape
    Kc = samples // PARTS
    C = Kc // cols
    me = lax.axis_index("cols")
    row = lax.axis_index("rows")
    chip, core = row // 2, lax.rem(row, 2)
    planes = 2
    ring = chips // planes
    plane, place = chip // ring, lax.rem(chip, ring)

    def col_of(k):
        return lax.rem(me + k, cols)

    def at_row(planes_on, places_on, cores_on):
        there = lax.rem(plane + planes_on, planes) * ring + lax.rem(place + places_on, ring)
        return there * 2 + lax.rem(core + cores_on, 2)

    def chunk(q, c):
        return pl.ds(pl.multiple_of((q * cols + c) * C, C), C)

    barrier = pltpu.get_barrier_semaphore()

    def greet(r, c):
        pl.semaphore_signal(barrier, inc=1, device_id=(r, c), device_id_type=MESH)

    for k in range(1, chips):
        greet(lax.rem(chip + k, chips) * 2 + core, me)
    for k in range(1, cols):
        greet(row, col_of(k))
        greet(at_row(1, 0, 0), col_of(k))
    for k in range(ring):
        greet(at_row(0, k, 1), me)

    small = [
        pltpu.make_async_copy(a, b, semI.at[n])
        for n, (a, b) in enumerate(
            [(sf_in, sf_ref), (thr_in, thr_ref), (leaf_in, leaf_ref), (base_in, base_ref), (labels_in, labels_ref), (node_in, node_ref)]
        )
    ]
    big = []
    for q in range(PARTS):
        at = pl.ds(q * Kc, Kc)
        big.append(pltpu.make_async_copy(codes_in.at[:, at], codes_ref.at[:, at], semC.at[q]))
    for copy in small[:2] + big + small[2:]:
        copy.start()

    i0 = lax.broadcasted_iota(jnp.int32, (128, 256), 0)
    i1 = lax.broadcasted_iota(jnp.int32, (128, 256), 1)
    same = (i0 // BINS) == ((i1 % 128) // BINS)
    sums[...] = jnp.where(same & ((i0 <= i1) | (i1 >= 128)), 1.0, 0.0)

    for copy in small[:2]:
        copy.wait()

    ids = lax.broadcasted_iota(jnp.int32, (feats, 256), 0) + me * feats
    low = lax.broadcasted_iota(jnp.int32, (16, 256), 0) == 0
    picks = jnp.concatenate(
        [jnp.where(sf_ref[...] == ids, 1.0, 0.0), jnp.where(low, -thr_ref[...].astype(F32), 0.0)], axis=0
    ).astype(BF16)

    def rows_of(slots):
        order = jnp.where(slots == lax.broadcasted_iota(jnp.int32, slots.shape, 1), 1.0, 0.0).astype(BF16)
        return lax.dot_general(order, picks, (((1,), (1,)), ((), ())), preferred_element_type=F32).astype(BF16)

    top = rows_of(lax.broadcasted_iota(jnp.int32, (SUB, 256), 0))

    ones = jnp.where(lax.broadcasted_iota(jnp.int32, (16, C), 0) == 0, 1.0, 0.0).astype(BF16)

    def cast(n, _):
        where = pl.ds(pl.multiple_of(n * C, C), C)
        aug[0:feats, where] = codes_ref[:, where].astype(BF16)
        aug[feats:, where] = ones
        return 0

    for q in range(PARTS):
        big[q].wait()
        lax.fori_loop(q * cols, (q + 1) * cols, cast, 0)

    pl.semaphore_wait(barrier, (chips - 1) + 2 * (cols - 1) + ring)

    def to_col(src, dst, sent, came, k):
        return pltpu.make_async_remote_copy(
            src_ref=src, dst_ref=dst, send_sem=sent, recv_sem=came, device_id=(row, col_of(k)), device_id_type=MESH
        )

    others = pl.ds(1, cols - 1)

    def top_bits(q, c):
        t = jnp.dot(top, aug[:, chunk(q, c)], preferred_element_type=F32)
        return jnp.where(t > 0.0, 1.0, 0.0).astype(BF16)

    def stepA(n, _):
        q, k = n // cols, lax.rem(n, cols)
        bits = top_bits(q, col_of(k))

        @pl.when(k > 0)
        def _():
            sA[q, k] = bits
            to_col(sA.at[q, k], rA.at[q, k], semA.at[0, q], semA.at[1, q], k).start()

        @pl.when(k == 0)
        def _():
            rA[q, 0] = bits

        return 0

    lax.fori_loop(0, PARTS * cols, stepA, 0)

    at = lax.broadcasted_iota(jnp.int32, (256, 256), 0)
    t, r = at // SUB, at % SUB
    width = jnp.where(r >= 8, 8, jnp.where(r >= 4, 4, jnp.where(r >= 2, 2, 1)))
    deep = rows_of((16 + t) * width + r - width)

    def table(n, _):
        where = pl.ds(pl.multiple_of(n * C, C), C)
        tab[:, where] = jnp.dot(deep, aug[:, where], preferred_element_type=F32).astype(BF16)
        return 0

    lax.fori_loop(0, PARTS * cols, table, 0)

    def total(ref, q):
        s = ref[q, 0].astype(F32)
        for k in range(1, cols):
            s = s + ref[q, k].astype(F32)
        return s

    def stepS(q, _):
        wait_bytes(rA.at[q, others], semA.at[1, q])
        subs[q, 0] = (walk(total(rA, q)) - SUB).astype(F32)
        for k in range(1, cols):
            to_col(subs.at[q, 0], subs.at[q, k], sentS.at[q], semS.at[q, k], k).start()
        return 0

    lax.fori_loop(0, PARTS, stepS, 0)

    def deep_bits(q, c, sub):
        sub = jnp.broadcast_to(sub, (SUB, C)).astype(BF16)
        got = jnp.zeros((SUB, C), BF16)
        for t in range(16):
            got = got + jnp.where(sub == BF16(t), tab[t * SUB : (t + 1) * SUB, chunk(q, c)], BF16(0))
        return jnp.where(got.astype(F32) > 0.0, 1.0, 0.0).astype(BF16)

    def stepB(n, _):
        q, k = n // cols, lax.rem(n, cols)
        back = lax.rem(cols - k, cols)

        @pl.when(k > 0)
        def _():
            wait_bytes(subs.at[q, k], semS.at[q, k])

        bits = deep_bits(q, col_of(back), subs[q, k])

        @pl.when(k > 0)
        def _():
            sB[q, back] = bits
            to_col(sB.at[q, back], rB.at[q, back], semB.at[0, q], semB.at[1, q], back).start()

        @pl.when(k == 0)
        def _():
            rB[q, 0] = bits

        return 0

    lax.fori_loop(0, PARTS * cols, stepB, 0)

    for copy in small[2:]:
        copy.wait()
    leaf = leaf_ref[...]
    high = leaf.astype(BF16).astype(F32)
    mid = (leaf - high).astype(BF16).astype(F32)
    rest = leaf - high - mid
    r16 = lax.broadcasted_iota(jnp.int32, (16, 256), 0)
    leaves = jnp.where(r16 == 0, high, jnp.where(r16 == 1, mid, jnp.where(r16 == 2, rest, 0.0))).astype(BF16)

    def narrow(n, _):
        where = pl.ds(pl.multiple_of(n * C, C), C)
        v8 = codes_ref[:, where].astype(I8)
        for g in range(chips):
            cs[g, :, where] = v8[GROUP * g : GROUP * (g + 1)]
        return 0

    lax.fori_loop(0, PARTS * cols, narrow, 0)

    def stepP(q, _):
        wait_bytes(rB.at[q, others], semB.at[1, q])
        slot = subs[q, 0].astype(jnp.int32) * 16 + walk(total(rB, q)) - SUB
        onehot = jnp.where(lax.broadcasted_iota(jnp.int32, (256, C), 0) == slot, 1.0, 0.0).astype(BF16)
        parts = jnp.dot(leaves, onehot, preferred_element_type=F32)
        weight = parts[0:1] + parts[1:2] + parts[2:3]
        ps[q, 0] = jax.nn.sigmoid(base_ref[q * cols + me] + weight)
        for k in range(1, cols):
            to_col(ps.at[q, 0], ps.at[q, k], sentP.at[q], semP.at[q, k], k).start()
        return 0

    lax.fori_loop(0, PARTS, stepP, 0)

    def weights(q, k, c):
        p = ps[q, k]
        n = q * cols + c
        gradient = (p - labels_ref[n].astype(F32)).astype(BF16).astype(F32)
        hessian = (p * (1.0 - p)).astype(BF16).astype(F32) * 4.0
        here = jnp.broadcast_to(node_ref[n].astype(F32), (NODES, C)).astype(BF16)
        node = here == lax.broadcasted_iota(jnp.int32, (NODES, C), 0).astype(F32).astype(BF16)
        for i, v in enumerate(pieces_of(jnp.concatenate([gradient, hessian], axis=0))):
            a = jnp.broadcast_to(v[0:1], (NODES, C)).astype(BF16)
            b = jnp.broadcast_to(v[1:2], (NODES, C)).astype(BF16)
            both = jnp.concatenate([jnp.where(node, a, BF16(0)), jnp.where(node, b, BF16(0))], axis=0)
            W[i * 32 : (i + 1) * 32, chunk(q, c)] = both.astype(F8)

    def stepW(n, _):
        q, k = n // cols, lax.rem(n, cols)

        @pl.when(k > 0)
        def _():
            wait_bytes(ps.at[q, k], semP.at[q, k])

        weights(q, k, col_of(lax.rem(cols - k, cols)))
        return 0

    lax.fori_loop(0, PARTS * cols, stepW, 0)

    def chip_of(i):
        j, far = lax.rem(i, ring), 1 - i // ring
        odd = lax.rem(j, 2)
        dz = odd * (ring // 2 - (j + 1) // 2) + (1 - odd) * (ring // 2 + j // 2)
        return lax.rem(plane + far, planes) * ring + lax.rem(place + dz, ring)

    def pair(i):
        return pltpu.make_async_remote_copy(
            src_ref=pair_s.at[i], dst_ref=pair_r.at[i], send_sem=sentX.at[0], recv_sem=semX.at[i],
            device_id=(chip * 2 + 1 - core, me), device_id_type=MESH,
        )

    def share(i):
        return pltpu.make_async_remote_copy(
            src_ref=hs.at[i], dst_ref=hr.at[i], send_sem=semH.at[0], recv_sem=semH.at[1],
            device_id=(chip_of(i) * 2 + core, me), device_id_type=MESH,
        )

    bins = lax.broadcasted_iota(jnp.int32, (BINS, samples), 0).astype(I8)

    def blocks(n):
        onehot = jnp.concatenate(
            [
                jnp.where(
                    jnp.broadcast_to(cs[g, f : f + 1, :], (BINS, samples)) == bins, jnp.ones((), F8), jnp.zeros((), F8)
                )
                for g in (chip_of(2 * n), chip_of(2 * n + 1))
                for f in range(GROUP)
            ],
            axis=0,
        )
        acc = lax.dot_general(W[...], onehot, (((1,), (1,)), ((), ())), preferred_element_type=F32)
        out = acc[0:32] * PIECE_SCALES[0]
        for p in range(1, PIECES):
            out = out + acc[p * 32 : (p + 1) * 32] * PIECE_SCALES[p]
        out = jnp.concatenate([out[0:16], out[16:32] * 0.25], axis=0)
        first = core == 0
        for h in range(2):
            left, right = out[:, 256 * h : 256 * h + 128], out[:, 256 * h + 128 : 256 * h + 256]
            hs[2 * n + h] = jnp.where(first, left, right)
            pair_s[2 * n + h] = jnp.where(first, right, left)
            pair(2 * n + h).start()

    def merge(i):
        wait_bytes(pair_r.at[i], semX.at[i])
        hs[i] = hs[i] + pair_r[i]

    def stepH(n, _):
        blocks(n)

        @pl.when(n > 0)
        def _():
            for i in (2 * n - 2, 2 * n - 1):
                merge(i)
                share(i).start()

        return 0

    lax.fori_loop(0, chips // 2, stepH, 0)
    merge(chips - 2)
    share(chips - 2).start()
    merge(chips - 1)
    wait_bytes(hr.at[pl.ds(0, chips - 1)], semH.at[1])
    hist = hs[chips - 1]
    for i in range(chips - 1):
        hist = hist + hr[i]

    both = jnp.dot(hist, sums[...], precision=lax.Precision.HIGHEST, preferred_element_type=F32)
    left, node = both[:, 0:128], both[:, 128:256]
    right = node - left

    def score(s):
        return s[0:16] * s[0:16] / (s[16:32] + reg_lambda)

    gains = 0.5 * (score(left) + score(right) - score(node))
    out_ref[0:NODES, :] = gains

    best = jnp.max(gains, axis=1, keepdims=True)
    d0 = lax.broadcasted_iota(jnp.int32, (16, 128), 0)
    d1 = lax.broadcasted_iota(jnp.int32, (16, 128), 1)
    best = jnp.max(jnp.where(d0 == d1, best, -jnp.inf), axis=0, keepdims=True)

    def exchange(n, src, got, sem, device, best):
        src[...] = best
        for k in range(1, n):
            pltpu.make_async_remote_copy(
                src_ref=src, dst_ref=got.at[k], send_sem=sem.at[0], recv_sem=sem.at[1],
                device_id=device(k), device_id_type=MESH,
            ).start()
        wait_bytes(got.at[pl.ds(1, n - 1)], sem.at[1])
        for k in range(1, n):
            best = jnp.maximum(best, got[k])
        return best

    best = exchange(2 * ring, m1s, m1r, semM, lambda k: (at_row(0, k % ring, k // ring), me), best)
    best = exchange(planes * cols, m2s, m2r, semN, lambda k: (at_row(k // cols, 0, 0), col_of(k % cols)), best)
    out_ref[NODES:, :] = jnp.broadcast_to(best, (8, 128))

    for q in range(PARTS):
        wait_bytes(sA.at[q, others], semA.at[0, q])
        wait_bytes(sB.at[q, others], semB.at[0, q])
        wait_bytes(subs.at[q, others], sentS.at[q])
        wait_bytes(ps.at[q, others], sentP.at[q])
    wait_bytes(pair_s, sentX.at[0])
    wait_bytes(hs.at[pl.ds(0, chips - 1)], semH.at[0])
    wait_bytes(m1r.at[pl.ds(1, 2 * ring - 1)], semM.at[0])
    wait_bytes(m2r.at[pl.ds(1, planes * cols - 1)], semN.at[0])


def finish(both_ref, gains_ref, best_ref):
    gains_ref[...] = both_ref[0:NODES]
    best_ref[...] = both_ref[NODES : NODES + 1, 0:NODES]


def shards(cols, rows, codes, labels, base_margin, node_id, split_feature, threshold, leaf_value):
    feats, samples = codes.shape
    chips = rows // 2
    C = samples // (cols * PARTS)
    vm = pl.BlockSpec(memory_space=pltpu.VMEM)
    anywhere = pl.BlockSpec(memory_space=pl.ANY)
    I32 = jnp.int32
    dma = pltpu.SemaphoreType.DMA
    by_chunk = lambda a: a.reshape(cols * PARTS, 1, C)
    out = pl.pallas_call(
        functools.partial(kernel, cols, chips),
        out_shape=jax.ShapeDtypeStruct((NODES + 8, 128), F32),
        in_specs=[anywhere] * 7,
        out_specs=vm,
        scratch_shapes=[
            pltpu.VMEM((feats, samples), I32),
            pltpu.VMEM((cols * PARTS, 1, C), I32),
            pltpu.VMEM((cols * PARTS, 1, C), F32),
            pltpu.VMEM((cols * PARTS, 1, C), I32),
            pltpu.VMEM((1, 256), I32),
            pltpu.VMEM((1, 256), I32),
            pltpu.VMEM((1, 256), F32),
            pltpu.VMEM((128, 256), F32),
            pltpu.VMEM((feats + 16, samples), BF16),
            pltpu.VMEM((chips, GROUP, samples), I8),
            pltpu.VMEM((256, samples), BF16),
            pltpu.VMEM((PARTS, cols, SUB, C), BF16),
            pltpu.VMEM((PARTS, cols, SUB, C), BF16),
            pltpu.VMEM((PARTS, cols, SUB, C), BF16),
            pltpu.VMEM((PARTS, cols, SUB, C), BF16),
            pltpu.VMEM((PARTS, cols, 1, C), F32),
            pltpu.VMEM((PARTS, cols, 1, C), F32),
            pltpu.VMEM((32 * PIECES, samples), F8),
            pltpu.VMEM((chips, 32, 128), F32),
            pltpu.VMEM((chips, 32, 128), F32),
            pltpu.VMEM((chips, 32, 128), F32),
            pltpu.VMEM((chips, 32, 128), F32),
            pltpu.VMEM((1, 128), F32),
            pltpu.VMEM((chips, 1, 128), F32),
            pltpu.VMEM((1, 128), F32),
            pltpu.VMEM((2 * cols, 1, 128), F32),
            dma((2, PARTS)),
            dma((PARTS, cols)),
            dma((2, PARTS)),
            dma((PARTS, cols)),
            dma((PARTS,)),
            dma((PARTS,)),
            dma((chips,)),
            dma((1,)),
            dma((2,)),
            dma((2,)),
            dma((2,)),
            dma((PARTS,)),
            dma((6,)),
        ],
        compiler_params=pltpu.CompilerParams(
            collective_id=0, has_side_effects=True, vmem_limit_bytes=56 * 2**20
        ),
        cost_estimate=pl.CostEstimate(
            flops=2 * 256 * samples * feats * BINS, bytes_accessed=4 * feats * samples, transcendentals=samples
        ),
    )(
        codes, by_chunk(labels), by_chunk(base_margin), by_chunk(node_id),
        split_feature.reshape(1, 256), threshold.reshape(1, 256), leaf_value.reshape(1, 256),
    )
    gains, best = pl.pallas_call(
        finish,
        out_shape=(jax.ShapeDtypeStruct((NODES, 128), F32), jax.ShapeDtypeStruct((1, NODES), F32)),
        in_specs=[vm],
        out_specs=(vm, vm),
    )(out)
    return gains, best.reshape(NODES)


def solution(mesh):
    return jax.shard_map(
        functools.partial(shards, mesh.shape["cols"], mesh.shape["rows"]),
        mesh=mesh,
        in_specs=(P("cols", "rows"), P("rows"), P("rows"), P("rows"), P(), P(), P()),
        out_specs=(P(None, ("cols", "rows")), P()),
        check_vma=False,
    )
```

```python
import functools

import jax
import jax.numpy as jnp
from jax import lax
from jax.experimental import pallas as pl
from jax.experimental.pallas import tpu as pltpu
from jax.sharding import PartitionSpec as P

BINS = 64
NODES = 16
SUB = 16
PIECES = 8
GROUP = 4
PARTS = 2
reg_lambda = 1.0
MESH = pl.DeviceIdType.MESH
F32, BF16, F8, I8 = jnp.float32, jnp.bfloat16, jnp.float8_e4m3fn, jnp.int8
PIECE_SCALES = [4.0**i / 2048.0 for i in range(6)] + [2.0**-19, 2.0**-23]


def walk(bits):
    rows = lax.broadcasted_iota(jnp.int32, bits.shape, 0)
    slot = jnp.ones((1, bits.shape[1]), jnp.int32)
    for _ in range(4):
        bit = jnp.sum(jnp.where(rows == slot, bits, 0.0), axis=0, keepdims=True)
        slot = 2 * slot + bit.astype(jnp.int32)
    return slot


def pieces_of(value):
    scaled = value * 2048.0
    whole = jnp.floor(scaled + 0.5)
    rest = (scaled - whole) * 256.0
    digits = []
    for _ in range(5):
        upper = jnp.floor(whole * 0.25 + 0.5)
        digits.append(whole - 4.0 * upper)
        whole = upper
    digits.append(whole)
    wide = rest * 1048577.0
    top = wide - (wide - rest)
    return digits + [top, (rest - top) * 16.0]


def wait_bytes(ref, sem):
    pltpu.make_async_copy(ref, ref, sem).wait()


def kernel(
    cols, chips,
    codes_in, labels_in, base_in, node_in, sf_in, thr_in, leaf_in,
    out_ref,
    codes_ref, labels_ref, base_ref, node_ref, sf_ref, thr_ref, leaf_ref, sums,
    aug, cs, tab, sA, rA, sB, rB, subs, ps, W, pair_s, pair_r, hs, hr, m1s, m1r, m2s, m2r,
    semA, semS, semB, semP, sentS, sentP, semX, sentX, semH, semM, semN, semC, semI,
):
    feats, samples = codes_ref.shape
    Kc = samples // PARTS
    C = Kc // cols
    me = lax.axis_index("cols")
    row = lax.axis_index("rows")
    chip, core = row // 2, lax.rem(row, 2)
    planes = 2
    ring = chips // planes
    plane, place = chip // ring, lax.rem(chip, ring)

    def col_of(k):
        return lax.rem(me + k, cols)

    def at_row(planes_on, places_on, cores_on):
        there = lax.rem(plane + planes_on, planes) * ring + lax.rem(place + places_on, ring)
        return there * 2 + lax.rem(core + cores_on, 2)

    def chunk(q, c):
        return pl.ds(pl.multiple_of((q * cols + c) * C, C), C)

    small = [
        pltpu.make_async_copy(a, b, semI.at[n])
        for n, (a, b) in enumerate(
            [(sf_in, sf_ref), (thr_in, thr_ref), (leaf_in, leaf_ref), (base_in, base_ref), (labels_in, labels_ref), (node_in, node_ref)]
        )
    ]
    big = []
    for q in range(PARTS):
        at = pl.ds(q * Kc, Kc)
        big.append(pltpu.make_async_copy(codes_in.at[:, at], codes_ref.at[:, at], semC.at[q]))
    for copy in small[:2] + big + small[2:]:
        copy.start()

    barrier = pltpu.get_barrier_semaphore()

    def greet(r, c):
        pl.semaphore_signal(barrier, inc=1, device_id=(r, c), device_id_type=MESH)

    for k in range(1, chips):
        greet(lax.rem(chip + k, chips) * 2 + core, me)
    for k in range(1, cols):
        greet(row, col_of(k))
        greet(at_row(1, 0, 0), col_of(k))
    for k in range(ring):
        greet(at_row(0, k, 1), me)

    i0 = lax.broadcasted_iota(jnp.int32, (128, 256), 0)
    i1 = lax.broadcasted_iota(jnp.int32, (128, 256), 1)
    same = (i0 // BINS) == ((i1 % 128) // BINS)
    sums[...] = jnp.where(same & ((i0 <= i1) | (i1 >= 128)), 1.0, 0.0).astype(BF16)

    for copy in small[:2]:
        copy.wait()

    ids = lax.broadcasted_iota(jnp.int32, (feats, 256), 0) + me * feats
    low = lax.broadcasted_iota(jnp.int32, (16, 256), 0) == 0
    picks = jnp.concatenate(
        [jnp.where(sf_ref[...] == ids, 1.0, 0.0), jnp.where(low, -thr_ref[...].astype(F32), 0.0)], axis=0
    ).astype(BF16)

    def rows_of(slots):
        order = jnp.where(slots == lax.broadcasted_iota(jnp.int32, slots.shape, 1), 1.0, 0.0).astype(BF16)
        return lax.dot_general(order, picks, (((1,), (1,)), ((), ())), preferred_element_type=F32).astype(BF16)

    top = rows_of(lax.broadcasted_iota(jnp.int32, (SUB, 256), 0))

    ones = jnp.where(lax.broadcasted_iota(jnp.int32, (16, C), 0) == 0, 1.0, 0.0).astype(BF16)

    def cast(n, _):
        where = pl.ds(pl.multiple_of(n * C, C), C)
        aug[0:feats, where] = codes_ref[:, where].astype(BF16)
        aug[feats:, where] = ones
        return 0

    for q in range(PARTS):
        big[q].wait()
        lax.fori_loop(q * cols, (q + 1) * cols, cast, 0)

    pl.semaphore_wait(barrier, (chips - 1) + 2 * (cols - 1) + ring)

    def to_col(src, dst, sent, came, k):
        return pltpu.make_async_remote_copy(
            src_ref=src, dst_ref=dst, send_sem=sent, recv_sem=came, device_id=(row, col_of(k)), device_id_type=MESH
        )

    others = pl.ds(1, cols - 1)

    def top_bits(q, c):
        t = jnp.dot(top, aug[:, chunk(q, c)], preferred_element_type=F32)
        return jnp.where(t > 0.0, 1.0, 0.0).astype(BF16)

    def stepA(n, _):
        q, k = n // cols, lax.rem(n, cols)
        bits = top_bits(q, col_of(k))

        @pl.when(k > 0)
        def _():
            sA[q, k] = bits
            to_col(sA.at[q, k], rA.at[q, k], semA.at[0, q], semA.at[1, q], k).start()

        @pl.when(k == 0)
        def _():
            rA[q, 0] = bits

        return 0

    lax.fori_loop(0, PARTS * cols, stepA, 0)

    at = lax.broadcasted_iota(jnp.int32, (256, 256), 0)
    t, r = at // SUB, at % SUB
    width = jnp.where(r >= 8, 8, jnp.where(r >= 4, 4, jnp.where(r >= 2, 2, 1)))
    deep = rows_of((16 + t) * width + r - width)

    def table(n, _):
        where = pl.ds(pl.multiple_of(n * C, C), C)
        tab[:, where] = jnp.dot(deep, aug[:, where], preferred_element_type=F32).astype(BF16)
        return 0

    lax.fori_loop(0, PARTS * cols, table, 0)

    def total(ref, q):
        s = ref[q, 0].astype(F32)
        for k in range(1, cols):
            s = s + ref[q, k].astype(F32)
        return s

    def stepS(q, _):
        wait_bytes(rA.at[q, others], semA.at[1, q])
        subs[q, 0] = (walk(total(rA, q)) - SUB).astype(F32)
        for k in range(1, cols):
            to_col(subs.at[q, 0], subs.at[q, k], sentS.at[q], semS.at[q, k], k).start()
        return 0

    lax.fori_loop(0, PARTS, stepS, 0)

    def deep_bits(q, c, sub):
        sub = jnp.broadcast_to(sub, (SUB, C)).astype(BF16)
        got = jnp.zeros((SUB, C), BF16)
        for t in range(16):
            got = got + jnp.where(sub == BF16(t), tab[t * SUB : (t + 1) * SUB, chunk(q, c)], BF16(0))
        return jnp.where(got.astype(F32) > 0.0, 1.0, 0.0).astype(BF16)

    def stepB(n, _):
        q, k = n // cols, lax.rem(n, cols)
        back = lax.rem(cols - k, cols)

        @pl.when(k > 0)
        def _():
            wait_bytes(subs.at[q, k], semS.at[q, k])

        bits = deep_bits(q, col_of(back), subs[q, k])

        @pl.when(k > 0)
        def _():
            sB[q, back] = bits
            to_col(sB.at[q, back], rB.at[q, back], semB.at[0, q], semB.at[1, q], back).start()

        @pl.when(k == 0)
        def _():
            rB[q, 0] = bits

        return 0

    lax.fori_loop(0, PARTS * cols, stepB, 0)

    for copy in small[2:]:
        copy.wait()
    leaf = leaf_ref[...]
    high = leaf.astype(BF16).astype(F32)
    mid = (leaf - high).astype(BF16).astype(F32)
    rest = leaf - high - mid
    r16 = lax.broadcasted_iota(jnp.int32, (16, 256), 0)
    leaves = jnp.where(r16 == 0, high, jnp.where(r16 == 1, mid, jnp.where(r16 == 2, rest, 0.0))).astype(BF16)

    def narrow(n, _):
        where = pl.ds(pl.multiple_of(n * C, C), C)
        v8 = codes_ref[:, where].astype(I8)
        for g in range(chips):
            cs[g, :, where] = v8[GROUP * g : GROUP * (g + 1)]
        return 0

    lax.fori_loop(0, PARTS * cols, narrow, 0)

    def stepP(q, _):
        wait_bytes(rB.at[q, others], semB.at[1, q])
        slot = subs[q, 0].astype(jnp.int32) * 16 + walk(total(rB, q)) - SUB
        onehot = jnp.where(lax.broadcasted_iota(jnp.int32, (256, C), 0) == slot, 1.0, 0.0).astype(BF16)
        parts = jnp.dot(leaves, onehot, preferred_element_type=F32)
        weight = parts[0:1] + parts[1:2] + parts[2:3]
        ps[q, 0] = jax.nn.sigmoid(base_ref[q * cols + me] + weight)
        for k in range(1, cols):
            to_col(ps.at[q, 0], ps.at[q, k], sentP.at[q], semP.at[q, k], k).start()
        return 0

    lax.fori_loop(0, PARTS, stepP, 0)

    def weights(q, k, c):
        p = ps[q, k]
        n = q * cols + c
        gradient = (p - labels_ref[n].astype(F32)).astype(BF16).astype(F32)
        hessian = (p * (1.0 - p)).astype(BF16).astype(F32) * 4.0
        here = jnp.broadcast_to(node_ref[n].astype(F32), (NODES, C)).astype(BF16)
        node = here == lax.broadcasted_iota(jnp.int32, (NODES, C), 0).astype(F32).astype(BF16)
        for i, v in enumerate(pieces_of(jnp.concatenate([gradient, hessian], axis=0))):
            a = jnp.broadcast_to(v[0:1], (NODES, C)).astype(BF16)
            b = jnp.broadcast_to(v[1:2], (NODES, C)).astype(BF16)
            both = jnp.concatenate([jnp.where(node, a, BF16(0)), jnp.where(node, b, BF16(0))], axis=0)
            W[i * 32 : (i + 1) * 32, chunk(q, c)] = both.astype(F8)

    def stepW(n, _):
        q, k = n // cols, lax.rem(n, cols)

        @pl.when(k > 0)
        def _():
            wait_bytes(ps.at[q, k], semP.at[q, k])

        weights(q, k, col_of(lax.rem(cols - k, cols)))
        return 0

    lax.fori_loop(0, PARTS * cols, stepW, 0)

    def chip_of(i):
        j, far = lax.rem(i, ring), 1 - i // ring
        odd = lax.rem(j, 2)
        dz = odd * (ring // 2 - (j + 1) // 2) + (1 - odd) * (ring // 2 + j // 2)
        return lax.rem(plane + far, planes) * ring + lax.rem(place + dz, ring)

    def pair(i):
        return pltpu.make_async_remote_copy(
            src_ref=pair_s.at[i], dst_ref=pair_r.at[i], send_sem=sentX.at[0], recv_sem=semX.at[i],
            device_id=(chip * 2 + 1 - core, me), device_id_type=MESH,
        )

    def share(i):
        return pltpu.make_async_remote_copy(
            src_ref=hs.at[i], dst_ref=hr.at[i], send_sem=semH.at[0], recv_sem=semH.at[1],
            device_id=(chip_of(i) * 2 + core, me), device_id_type=MESH,
        )

    bins = lax.broadcasted_iota(jnp.int32, (BINS, samples), 0).astype(I8)

    def blocks(n):
        onehot = jnp.concatenate(
            [
                jnp.where(
                    jnp.broadcast_to(cs[g, f : f + 1, :], (BINS, samples)) == bins, jnp.ones((), F8), jnp.zeros((), F8)
                )
                for g in (chip_of(2 * n), chip_of(2 * n + 1))
                for f in range(GROUP)
            ],
            axis=0,
        )
        acc = lax.dot_general(W[...], onehot, (((1,), (1,)), ((), ())), preferred_element_type=F32)
        out = acc[0:32] * PIECE_SCALES[0]
        for p in range(1, PIECES):
            out = out + acc[p * 32 : (p + 1) * 32] * PIECE_SCALES[p]
        out = jnp.concatenate([out[0:16], out[16:32] * 0.25], axis=0)
        first = core == 0
        for h in range(2):
            left, right = out[:, 256 * h : 256 * h + 128], out[:, 256 * h + 128 : 256 * h + 256]
            hs[2 * n + h] = jnp.where(first, left, right)
            pair_s[2 * n + h] = jnp.where(first, right, left)

        @pl.when(n < chips // 2 - 1)
        def _():
            pair(2 * n).start()

        pair(2 * n + 1).start()


    def across():
        return pltpu.make_async_remote_copy(
            src_ref=pair_s.at[chips - 2], dst_ref=hr.at[chips - 1], send_sem=semH.at[0], recv_sem=semH.at[1],
            device_id=(chip_of(chips - 2) * 2 + 1 - core, me), device_id_type=MESH,
        )

    def merge(i):
        wait_bytes(pair_r.at[i], semX.at[i])
        hs[i] = hs[i] + pair_r[i]

    def stepH(n, _):
        blocks(n)

        @pl.when(n == chips // 2 - 1)
        def _():
            share(chips - 2).start()
            across().start()

        @pl.when(n > 0)
        def _():
            for i in (2 * n - 2, 2 * n - 1):
                merge(i)
                share(i).start()

        return 0

    lax.fori_loop(0, chips // 2, stepH, 0)
    merge(chips - 1)
    wait_bytes(hr, semH.at[1])
    hist = hs[chips - 1]
    for i in range(chips):
        hist = hist + hr[i]

    high = hist.astype(BF16).astype(F32)
    mid = (hist - high).astype(BF16).astype(F32)
    three = jnp.concatenate([high, mid, hist - high - mid], axis=0).astype(BF16)
    three = jnp.dot(three, sums[...], preferred_element_type=F32)
    both = three[0:32] + (three[32:64] + three[64:96])
    left, node = both[:, 0:128], both[:, 128:256]
    right = node - left

    def score(s):
        return s[0:16] * s[0:16] / (s[16:32] + reg_lambda)

    gains = 0.5 * (score(left) + score(right) - score(node))
    out_ref[0:NODES, :] = gains

    best = jnp.max(gains, axis=1, keepdims=True)
    d0 = lax.broadcasted_iota(jnp.int32, (16, 128), 0)
    d1 = lax.broadcasted_iota(jnp.int32, (16, 128), 1)
    best = jnp.max(jnp.where(d0 == d1, best, -jnp.inf), axis=0, keepdims=True)

    def exchange(n, src, got, sem, device, best):
        src[...] = best
        for k in range(1, n):
            pltpu.make_async_remote_copy(
                src_ref=src, dst_ref=got.at[k], send_sem=sem.at[0], recv_sem=sem.at[1],
                device_id=device(k), device_id_type=MESH,
            ).start()
        wait_bytes(got.at[pl.ds(1, n - 1)], sem.at[1])
        for k in range(1, n):
            best = jnp.maximum(best, got[k])
        return best

    best = exchange(2 * ring, m1s, m1r, semM, lambda k: (at_row(0, k % ring, k // ring), me), best)
    best = exchange(planes * cols, m2s, m2r, semN, lambda k: (at_row(k // cols, 0, 0), col_of(k % cols)), best)
    out_ref[NODES:, :] = jnp.broadcast_to(best, (8, 128))

    for q in range(PARTS):
        wait_bytes(sA.at[q, others], semA.at[0, q])
        wait_bytes(sB.at[q, others], semB.at[0, q])
        wait_bytes(subs.at[q, others], sentS.at[q])
        wait_bytes(ps.at[q, others], sentP.at[q])
    wait_bytes(pair_s.at[pl.ds(0, chips - 1)], sentX.at[0])
    wait_bytes(hs, semH.at[0])
    wait_bytes(m1r.at[pl.ds(1, 2 * ring - 1)], semM.at[0])
    wait_bytes(m2r.at[pl.ds(1, planes * cols - 1)], semN.at[0])


def finish(both_ref, gains_ref, best_ref):
    gains_ref[...] = both_ref[0:NODES]
    best_ref[...] = both_ref[NODES : NODES + 1, 0:NODES]


def shards(cols, rows, codes, labels, base_margin, node_id, split_feature, threshold, leaf_value):
    feats, samples = codes.shape
    chips = rows // 2
    C = samples // (cols * PARTS)
    vm = pl.BlockSpec(memory_space=pltpu.VMEM)
    anywhere = pl.BlockSpec(memory_space=pl.ANY)
    I32 = jnp.int32
    dma = pltpu.SemaphoreType.DMA
    by_chunk = lambda a: a.reshape(cols * PARTS, 1, C)
    out = pl.pallas_call(
        functools.partial(kernel, cols, chips),
        out_shape=jax.ShapeDtypeStruct((NODES + 8, 128), F32),
        in_specs=[anywhere] * 7,
        out_specs=vm,
        scratch_shapes=[
            pltpu.VMEM((feats, samples), I32),
            pltpu.VMEM((cols * PARTS, 1, C), I32),
            pltpu.VMEM((cols * PARTS, 1, C), F32),
            pltpu.VMEM((cols * PARTS, 1, C), I32),
            pltpu.VMEM((1, 256), I32),
            pltpu.VMEM((1, 256), I32),
            pltpu.VMEM((1, 256), F32),
            pltpu.VMEM((128, 256), BF16),
            pltpu.VMEM((feats + 16, samples), BF16),
            pltpu.VMEM((chips, GROUP, samples), I8),
            pltpu.VMEM((256, samples), BF16),
            pltpu.VMEM((PARTS, cols, SUB, C), BF16),
            pltpu.VMEM((PARTS, cols, SUB, C), BF16),
            pltpu.VMEM((PARTS, cols, SUB, C), BF16),
            pltpu.VMEM((PARTS, cols, SUB, C), BF16),
            pltpu.VMEM((PARTS, cols, 1, C), F32),
            pltpu.VMEM((PARTS, cols, 1, C), F32),
            pltpu.VMEM((32 * PIECES, samples), F8),
            pltpu.VMEM((chips, 32, 128), F32),
            pltpu.VMEM((chips, 32, 128), F32),
            pltpu.VMEM((chips, 32, 128), F32),
            pltpu.VMEM((chips, 32, 128), F32),
            pltpu.VMEM((1, 128), F32),
            pltpu.VMEM((chips, 1, 128), F32),
            pltpu.VMEM((1, 128), F32),
            pltpu.VMEM((2 * cols, 1, 128), F32),
            dma((2, PARTS)),
            dma((PARTS, cols)),
            dma((2, PARTS)),
            dma((PARTS, cols)),
            dma((PARTS,)),
            dma((PARTS,)),
            dma((chips,)),
            dma((1,)),
            dma((2,)),
            dma((2,)),
            dma((2,)),
            dma((PARTS,)),
            dma((6,)),
        ],
        compiler_params=pltpu.CompilerParams(
            collective_id=0, has_side_effects=True, vmem_limit_bytes=56 * 2**20
        ),
        cost_estimate=pl.CostEstimate(
            flops=2 * 256 * samples * feats * BINS, bytes_accessed=4 * feats * samples, transcendentals=samples
        ),
    )(
        codes, by_chunk(labels), by_chunk(base_margin), by_chunk(node_id),
        split_feature.reshape(1, 256), threshold.reshape(1, 256), leaf_value.reshape(1, 256),
    )
    gains, best = pl.pallas_call(
        finish,
        out_shape=(jax.ShapeDtypeStruct((NODES, 128), F32), jax.ShapeDtypeStruct((1, NODES), F32)),
        in_specs=[vm],
        out_specs=(vm, vm),
    )(out)
    return gains, best.reshape(NODES)


def solution(mesh):
    return jax.shard_map(
        functools.partial(shards, mesh.shape["cols"], mesh.shape["rows"]),
        mesh=mesh,
        in_specs=(P("cols", "rows"), P("rows"), P("rows"), P("rows"), P(), P(), P()),
        out_specs=(P(None, ("cols", "rows")), P()),
        check_vma=False,
    )
```

```python
import functools

import jax
import jax.numpy as jnp
from jax import lax
from jax.experimental import pallas as pl
from jax.experimental.pallas import tpu as pltpu
from jax.sharding import PartitionSpec as P

BINS = 64
NODES = 16
SUB = 16
PIECES = 8
GROUP = 4
PARTS = 2
reg_lambda = 1.0
MESH = pl.DeviceIdType.MESH
F32, BF16, F8, I8 = jnp.float32, jnp.bfloat16, jnp.float8_e4m3fn, jnp.int8
PIECE_SCALES = [4.0**i / 2048.0 for i in range(6)] + [2.0**-19, 2.0**-23]


def walk(bits):
    rows = lax.broadcasted_iota(jnp.int32, bits.shape, 0)
    slot = jnp.ones((1, bits.shape[1]), jnp.int32)
    for _ in range(4):
        bit = jnp.sum(jnp.where(rows == slot, bits, 0.0), axis=0, keepdims=True)
        slot = 2 * slot + bit.astype(jnp.int32)
    return slot


def pieces_of(value):
    scaled = value * 2048.0
    whole = jnp.floor(scaled + 0.5)
    rest = (scaled - whole) * 256.0
    digits = []
    for _ in range(5):
        upper = jnp.floor(whole * 0.25 + 0.5)
        digits.append(whole - 4.0 * upper)
        whole = upper
    digits.append(whole)
    wide = rest * 1048577.0
    top = wide - (wide - rest)
    return digits + [top, (rest - top) * 16.0]


def wait_bytes(ref, sem):
    pltpu.make_async_copy(ref, ref, sem).wait()


def kernel(
    cols, chips,
    codes_in, labels_in, base_in, node_in, sf_in, thr_in, leaf_in,
    out_ref,
    codes_ref, labels_ref, base_ref, node_ref, sf_ref, thr_ref, leaf_ref, sums,
    aug, cs, tab, sA, rA, sB, rB, subs, ps, W, pair_s, pair_r, hs, hr, m1s, m1r, m2s, m2r,
    semA, semS, semB, semP, sentS, sentP, semX, sentX, semH, semM, semN, semC, semI,
):
    feats, samples = codes_ref.shape
    Kc = samples // PARTS
    C = Kc // cols
    me = lax.axis_index("cols")
    row = lax.axis_index("rows")
    chip, core = row // 2, lax.rem(row, 2)
    planes = 2
    ring = chips // planes
    plane, place = chip // ring, lax.rem(chip, ring)

    def col_of(k):
        return lax.rem(me + k, cols)

    def at_row(planes_on, places_on, cores_on):
        there = lax.rem(plane + planes_on, planes) * ring + lax.rem(place + places_on, ring)
        return there * 2 + lax.rem(core + cores_on, 2)

    def chunk(q, c):
        return pl.ds(pl.multiple_of((q * cols + c) * C, C), C)

    small = [
        pltpu.make_async_copy(a, b, semI.at[n])
        for n, (a, b) in enumerate(
            [(sf_in, sf_ref), (thr_in, thr_ref), (leaf_in, leaf_ref), (base_in, base_ref), (labels_in, labels_ref), (node_in, node_ref)]
        )
    ]
    big = []
    for q in range(PARTS):
        at = pl.ds(q * Kc, Kc)
        big.append(pltpu.make_async_copy(codes_in.at[:, at], codes_ref.at[:, at], semC.at[q]))
    for copy in small[:2] + big + small[2:]:
        copy.start()

    barrier = pltpu.get_barrier_semaphore()

    def greet(r, c):
        pl.semaphore_signal(barrier, inc=1, device_id=(r, c), device_id_type=MESH)

    for k in range(1, chips):
        greet(lax.rem(chip + k, chips) * 2 + core, me)
    for k in range(1, cols):
        greet(row, col_of(k))
        greet(at_row(1, 0, 0), col_of(k))
    for k in range(ring):
        greet(at_row(0, k, 1), me)

    i0 = lax.broadcasted_iota(jnp.int32, (128, 256), 0)
    i1 = lax.broadcasted_iota(jnp.int32, (128, 256), 1)
    same = (i0 // BINS) == ((i1 % 128) // BINS)
    sums[...] = jnp.where(same & ((i0 <= i1) | (i1 >= 128)), 1.0, 0.0).astype(BF16)

    for copy in small[:2]:
        copy.wait()

    ids = lax.broadcasted_iota(jnp.int32, (feats, 256), 0) + me * feats
    low = lax.broadcasted_iota(jnp.int32, (16, 256), 0) == 0
    picks = jnp.concatenate(
        [jnp.where(sf_ref[...] == ids, 1.0, 0.0), jnp.where(low, -thr_ref[...].astype(F32), 0.0)], axis=0
    ).astype(BF16)

    def rows_of(slots):
        order = jnp.where(slots == lax.broadcasted_iota(jnp.int32, slots.shape, 1), 1.0, 0.0).astype(BF16)
        return lax.dot_general(order, picks, (((1,), (1,)), ((), ())), preferred_element_type=F32).astype(BF16)

    top = rows_of(lax.broadcasted_iota(jnp.int32, (SUB, 256), 0))

    ones = jnp.where(lax.broadcasted_iota(jnp.int32, (16, C), 0) == 0, 1.0, 0.0).astype(BF16)

    def cast(n, _):
        where = pl.ds(pl.multiple_of(n * C, C), C)
        aug[0:feats, where] = codes_ref[:, where].astype(BF16)
        aug[feats:, where] = ones
        return 0

    for q in range(PARTS):
        big[q].wait()
        lax.fori_loop(q * cols, (q + 1) * cols, cast, 0)

    pl.semaphore_wait(barrier, (chips - 1) + 2 * (cols - 1) + ring)

    def to_col(src, dst, sent, came, k):
        return pltpu.make_async_remote_copy(
            src_ref=src, dst_ref=dst, send_sem=sent, recv_sem=came, device_id=(row, col_of(k)), device_id_type=MESH
        )

    others = pl.ds(1, cols - 1)

    def top_bits(q, c):
        t = jnp.dot(top, aug[:, chunk(q, c)], preferred_element_type=F32)
        return jnp.where(t > 0.0, 1.0, 0.0).astype(BF16)

    def stepA(n, _):
        q, k = n // cols, lax.rem(n, cols)
        bits = top_bits(q, col_of(k))

        @pl.when(k > 0)
        def _():
            sA[q, k] = bits
            to_col(sA.at[q, k], rA.at[q, k], semA.at[0, q], semA.at[1, q], k).start()

        @pl.when(k == 0)
        def _():
            rA[q, 0] = bits

        return 0

    lax.fori_loop(0, PARTS * cols, stepA, 0)

    at = lax.broadcasted_iota(jnp.int32, (256, 256), 0)
    t, r = at // SUB, at % SUB
    width = jnp.where(r >= 8, 8, jnp.where(r >= 4, 4, jnp.where(r >= 2, 2, 1)))
    deep = rows_of((16 + t) * width + r - width)

    def table(n, _):
        where = pl.ds(pl.multiple_of(n * C, C), C)
        tab[:, where] = jnp.dot(deep, aug[:, where], preferred_element_type=F32).astype(BF16)
        return 0

    lax.fori_loop(0, PARTS * cols, table, 0)

    def total(ref, q):
        s = ref[q, 0].astype(F32)
        for k in range(1, cols):
            s = s + ref[q, k].astype(F32)
        return s

    def stepS(q, _):
        wait_bytes(rA.at[q, others], semA.at[1, q])
        subs[q, 0] = (walk(total(rA, q)) - SUB).astype(F32)
        for k in range(1, cols):
            to_col(subs.at[q, 0], subs.at[q, k], sentS.at[q], semS.at[q, k], k).start()
        return 0

    lax.fori_loop(0, PARTS, stepS, 0)

    def deep_bits(q, c, sub):
        sub = jnp.broadcast_to(sub, (SUB, C)).astype(BF16)
        got = jnp.zeros((SUB, C), BF16)
        for t in range(16):
            got = got + jnp.where(sub == BF16(t), tab[t * SUB : (t + 1) * SUB, chunk(q, c)], BF16(0))
        return jnp.where(got.astype(F32) > 0.0, 1.0, 0.0).astype(BF16)

    def stepB(n, _):
        q, k = n // cols, lax.rem(n, cols)
        back = lax.rem(cols - k, cols)

        @pl.when(k > 0)
        def _():
            wait_bytes(subs.at[q, k], semS.at[q, k])

        bits = deep_bits(q, col_of(back), subs[q, k])

        @pl.when(k > 0)
        def _():
            sB[q, back] = bits
            to_col(sB.at[q, back], rB.at[q, back], semB.at[0, q], semB.at[1, q], back).start()

        @pl.when(k == 0)
        def _():
            rB[q, 0] = bits

        return 0

    lax.fori_loop(0, PARTS * cols, stepB, 0)

    for copy in small[2:]:
        copy.wait()
    leaf = leaf_ref[...]
    high = leaf.astype(BF16).astype(F32)
    mid = (leaf - high).astype(BF16).astype(F32)
    rest = leaf - high - mid
    r16 = lax.broadcasted_iota(jnp.int32, (16, 256), 0)
    leaves = jnp.where(r16 == 0, high, jnp.where(r16 == 1, mid, jnp.where(r16 == 2, rest, 0.0))).astype(BF16)

    def narrow(n, _):
        where = pl.ds(pl.multiple_of(n * C, C), C)
        v8 = codes_ref[:, where].astype(I8)
        for g in range(chips):
            cs[g, :, where] = v8[GROUP * g : GROUP * (g + 1)]
        return 0

    lax.fori_loop(0, PARTS * cols, narrow, 0)

    def stepP(q, _):
        wait_bytes(rB.at[q, others], semB.at[1, q])
        slot = subs[q, 0].astype(jnp.int32) * 16 + walk(total(rB, q)) - SUB
        onehot = jnp.where(lax.broadcasted_iota(jnp.int32, (256, C), 0) == slot, 1.0, 0.0).astype(BF16)
        parts = jnp.dot(leaves, onehot, preferred_element_type=F32)
        weight = parts[0:1] + parts[1:2] + parts[2:3]
        ps[q, 0] = jax.nn.sigmoid(base_ref[q * cols + me] + weight)
        for k in range(1, cols):
            to_col(ps.at[q, 0], ps.at[q, k], sentP.at[q], semP.at[q, k], k).start()
        return 0

    lax.fori_loop(0, PARTS, stepP, 0)

    def weights(q, k, c):
        p = ps[q, k]
        n = q * cols + c
        gradient = (p - labels_ref[n].astype(F32)).astype(BF16).astype(F32)
        hessian = (p * (1.0 - p)).astype(BF16).astype(F32) * 4.0
        here = jnp.broadcast_to(node_ref[n].astype(F32), (NODES, C)).astype(BF16)
        node = here == lax.broadcasted_iota(jnp.int32, (NODES, C), 0).astype(F32).astype(BF16)
        for i, v in enumerate(pieces_of(jnp.concatenate([gradient, hessian], axis=0))):
            a = jnp.broadcast_to(v[0:1], (NODES, C)).astype(BF16)
            b = jnp.broadcast_to(v[1:2], (NODES, C)).astype(BF16)
            both = jnp.concatenate([jnp.where(node, a, BF16(0)), jnp.where(node, b, BF16(0))], axis=0)
            W[i * 32 : (i + 1) * 32, chunk(q, c)] = both.astype(F8)

    def stepW(n, _):
        q, k = n // cols, lax.rem(n, cols)

        @pl.when(k > 0)
        def _():
            wait_bytes(ps.at[q, k], semP.at[q, k])

        weights(q, k, col_of(lax.rem(cols - k, cols)))
        return 0

    lax.fori_loop(0, PARTS * cols, stepW, 0)

    def chip_of(i):
        j, far = lax.rem(i, ring), 1 - i // ring
        odd = lax.rem(j, 2)
        dz = odd * (ring // 2 - (j + 1) // 2) + (1 - odd) * (ring // 2 + j // 2)
        return lax.rem(plane + far, planes) * ring + lax.rem(place + dz, ring)

    def pair(i):
        return pltpu.make_async_remote_copy(
            src_ref=pair_s.at[i], dst_ref=pair_r.at[i], send_sem=sentX.at[0], recv_sem=semX.at[i],
            device_id=(chip * 2 + 1 - core, me), device_id_type=MESH,
        )

    def share(i):
        return pltpu.make_async_remote_copy(
            src_ref=hs.at[i], dst_ref=hr.at[i], send_sem=semH.at[0], recv_sem=semH.at[1],
            device_id=(chip_of(i) * 2 + core, me), device_id_type=MESH,
        )

    bins = lax.broadcasted_iota(jnp.int32, (BINS, samples), 0).astype(I8)

    def block(i):
        g = chip_of(i)
        onehot = jnp.concatenate(
            [
                jnp.where(
                    jnp.broadcast_to(cs[g, f : f + 1, :], (BINS, samples)) == bins, jnp.ones((), F8), jnp.zeros((), F8)
                )
                for f in range(GROUP)
            ],
            axis=0,
        )
        acc = lax.dot_general(W[...], onehot, (((1,), (1,)), ((), ())), preferred_element_type=F32)
        out = acc[0:32] * PIECE_SCALES[0]
        for n in range(1, PIECES):
            out = out + acc[n * 32 : (n + 1) * 32] * PIECE_SCALES[n]
        out = jnp.concatenate([out[0:16], out[16:32] * 0.25], axis=0)
        left, right = out[:, 0:128], out[:, 128:256]
        first = core == 0
        hs[i] = jnp.where(first, left, right)
        pair_s[i] = jnp.where(first, right, left)

        @pl.when(i != chips - 2)
        def _():
            pair(i).start()

        @pl.when(i == chips - 2)
        def _():
            share(i).start()
            across().start()


    def across():
        return pltpu.make_async_remote_copy(
            src_ref=pair_s.at[chips - 2], dst_ref=hr.at[chips - 1], send_sem=semH.at[0], recv_sem=semH.at[1],
            device_id=(chip_of(chips - 2) * 2 + 1 - core, me), device_id_type=MESH,
        )

    def merge(i):
        wait_bytes(pair_r.at[i], semX.at[i])
        hs[i] = hs[i] + pair_r[i]

    def stepH(i, _):
        block(i)

        @pl.when((i > 0) & (i < chips - 1))
        def _():
            merge(i - 1)
            share(i - 1).start()

        return 0

    lax.fori_loop(0, chips, stepH, 0)
    merge(chips - 1)
    wait_bytes(hr, semH.at[1])
    hist = hs[chips - 1]
    for i in range(chips):
        hist = hist + hr[i]

    high = hist.astype(BF16).astype(F32)
    mid = (hist - high).astype(BF16).astype(F32)
    three = jnp.concatenate([high, mid, hist - high - mid], axis=0).astype(BF16)
    three = jnp.dot(three, sums[...], preferred_element_type=F32)
    both = three[0:32] + (three[32:64] + three[64:96])
    left, node = both[:, 0:128], both[:, 128:256]
    right = node - left

    def score(s):
        return s[0:16] * s[0:16] / (s[16:32] + reg_lambda)

    gains = 0.5 * (score(left) + score(right) - score(node))
    out_ref[0:NODES, :] = gains

    best = jnp.max(gains, axis=1, keepdims=True)
    d0 = lax.broadcasted_iota(jnp.int32, (16, 128), 0)
    d1 = lax.broadcasted_iota(jnp.int32, (16, 128), 1)
    best = jnp.max(jnp.where(d0 == d1, best, -jnp.inf), axis=0, keepdims=True)

    def exchange(n, src, got, sem, device, best):
        src[...] = best
        for k in range(1, n):
            pltpu.make_async_remote_copy(
                src_ref=src, dst_ref=got.at[k], send_sem=sem.at[0], recv_sem=sem.at[1],
                device_id=device(k), device_id_type=MESH,
            ).start()
        wait_bytes(got.at[pl.ds(1, n - 1)], sem.at[1])
        for k in range(1, n):
            best = jnp.maximum(best, got[k])
        return best

    best = exchange(2 * ring, m1s, m1r, semM, lambda k: (at_row(0, k % ring, k // ring), me), best)
    best = exchange(planes * cols, m2s, m2r, semN, lambda k: (at_row(k // cols, 0, 0), col_of(k % cols)), best)
    out_ref[NODES:, :] = jnp.broadcast_to(best, (8, 128))

    for q in range(PARTS):
        wait_bytes(sA.at[q, others], semA.at[0, q])
        wait_bytes(sB.at[q, others], semB.at[0, q])
        wait_bytes(subs.at[q, others], sentS.at[q])
        wait_bytes(ps.at[q, others], sentP.at[q])
    wait_bytes(pair_s.at[pl.ds(0, chips - 1)], sentX.at[0])
    wait_bytes(hs, semH.at[0])
    wait_bytes(m1r.at[pl.ds(1, 2 * ring - 1)], semM.at[0])
    wait_bytes(m2r.at[pl.ds(1, planes * cols - 1)], semN.at[0])


def finish(both_ref, gains_ref, best_ref):
    gains_ref[...] = both_ref[0:NODES]
    best_ref[...] = both_ref[NODES : NODES + 1, 0:NODES]


def shards(cols, rows, codes, labels, base_margin, node_id, split_feature, threshold, leaf_value):
    feats, samples = codes.shape
    chips = rows // 2
    C = samples // (cols * PARTS)
    vm = pl.BlockSpec(memory_space=pltpu.VMEM)
    anywhere = pl.BlockSpec(memory_space=pl.ANY)
    I32 = jnp.int32
    dma = pltpu.SemaphoreType.DMA
    by_chunk = lambda a: a.reshape(cols * PARTS, 1, C)
    out = pl.pallas_call(
        functools.partial(kernel, cols, chips),
        out_shape=jax.ShapeDtypeStruct((NODES + 8, 128), F32),
        in_specs=[anywhere] * 7,
        out_specs=vm,
        scratch_shapes=[
            pltpu.VMEM((feats, samples), I32),
            pltpu.VMEM((cols * PARTS, 1, C), I32),
            pltpu.VMEM((cols * PARTS, 1, C), F32),
            pltpu.VMEM((cols * PARTS, 1, C), I32),
            pltpu.VMEM((1, 256), I32),
            pltpu.VMEM((1, 256), I32),
            pltpu.VMEM((1, 256), F32),
            pltpu.VMEM((128, 256), BF16),
            pltpu.VMEM((feats + 16, samples), BF16),
            pltpu.VMEM((chips, GROUP, samples), I8),
            pltpu.VMEM((256, samples), BF16),
            pltpu.VMEM((PARTS, cols, SUB, C), BF16),
            pltpu.VMEM((PARTS, cols, SUB, C), BF16),
            pltpu.VMEM((PARTS, cols, SUB, C), BF16),
            pltpu.VMEM((PARTS, cols, SUB, C), BF16),
            pltpu.VMEM((PARTS, cols, 1, C), F32),
            pltpu.VMEM((PARTS, cols, 1, C), F32),
            pltpu.VMEM((32 * PIECES, samples), F8),
            pltpu.VMEM((chips, 32, 128), F32),
            pltpu.VMEM((chips, 32, 128), F32),
            pltpu.VMEM((chips, 32, 128), F32),
            pltpu.VMEM((chips, 32, 128), F32),
            pltpu.VMEM((1, 128), F32),
            pltpu.VMEM((chips, 1, 128), F32),
            pltpu.VMEM((1, 128), F32),
            pltpu.VMEM((2 * cols, 1, 128), F32),
            dma((2, PARTS)),
            dma((PARTS, cols)),
            dma((2, PARTS)),
            dma((PARTS, cols)),
            dma((PARTS,)),
            dma((PARTS,)),
            dma((chips,)),
            dma((1,)),
            dma((2,)),
            dma((2,)),
            dma((2,)),
            dma((PARTS,)),
            dma((6,)),
        ],
        compiler_params=pltpu.CompilerParams(
            collective_id=0, has_side_effects=True, vmem_limit_bytes=56 * 2**20
        ),
        cost_estimate=pl.CostEstimate(
            flops=2 * 256 * samples * feats * BINS, bytes_accessed=4 * feats * samples, transcendentals=samples
        ),
    )(
        codes, by_chunk(labels), by_chunk(base_margin), by_chunk(node_id),
        split_feature.reshape(1, 256), threshold.reshape(1, 256), leaf_value.reshape(1, 256),
    )
    gains, best = pl.pallas_call(
        finish,
        out_shape=(jax.ShapeDtypeStruct((NODES, 128), F32), jax.ShapeDtypeStruct((1, NODES), F32)),
        in_specs=[vm],
        out_specs=(vm, vm),
    )(out)
    return gains, best.reshape(NODES)


def solution(mesh):
    return jax.shard_map(
        functools.partial(shards, mesh.shape["cols"], mesh.shape["rows"]),
        mesh=mesh,
        in_specs=(P("cols", "rows"), P("rows"), P("rows"), P("rows"), P(), P(), P()),
        out_specs=(P(None, ("cols", "rows")), P()),
        check_vma=False,
    )
```
